128 devices in a mesh: au: 8 (over y, z_hi), vert: 16 (over x, z_lo, core).
Axes of the slice: x: 4, y: 4, z: 4 (z_hi: 2, z_lo: 2; z = z_hi * 2 + z_lo), core: 2. Of those that a mesh axis runs over, the one named last changes fastest.
Arguments:
- u_band: float32 [16384, 8192], P(('au', 'vert')), may hold values from -6 to 6
- v_band: float32 [16384, 8192], P(('vert', 'au')), may hold values from -6 to 6
- y_left: float32 [4, 16384, 128], P(None, ('au', 'vert')), may hold values from -0.046875 to 0.046875
- t_left: float32 [4, 128, 128], replicated, may hold values from -3 to 3
- y_right: float32 [4, 16384, 128], P(None, ('vert', 'au')), may hold values from -0.046875 to 0.046875
- t_right: float32 [4, 128, 128], replicated, may hold values from -3 to 3
Outputs:
- u_out: float32 [16384, 8192], P('au', 'vert')
- v_out: float32 [16384, 8192], P('vert', 'au')
The draws below stay inside these ranges and needn't reach their ends.
All inputs are finite; a program needn't handle non-finite values.
Results may differ from the reference program's by a relative error of at most 0.0001.
Values sent between devices are 32-bit elements; how exact they have to be, the bound alone decides.
A program may use at most 128 MiB of HBM per device.

```python
import jax
import jax.numpy as jnp
from jax import lax

K = 8192
NB = 128
PANELS = 4
MROWS = 16384


def block_scale(stream_key, extent, split, low, largest):
    def one(dim, parts):
        draws = jax.random.uniform(jax.random.fold_in(jax.random.fold_in(stream_key, 6), dim), (parts,), jnp.float32, low / len(split), largest / len(split))
        return jnp.repeat(jnp.exp(draws), extent[dim] // parts).reshape((-1,) + (1,) * (len(extent) - dim - 1))

    factor_of = one(*split[0])
    for cut in split[1:]:
        factor_of = factor_of * one(*cut)
    return factor_of


def noise(stream_key, extent, spread, limit, cuts=(), held_as=jnp.bfloat16):
    loudness = block_scale(stream_key, extent, cuts, -0.22, 0.18) if cuts else 1.0
    drawn = jax.random.normal(stream_key, extent, jnp.float32) * spread * loudness
    return jnp.minimum(jnp.maximum(drawn, -limit), limit).astype(held_as)


def setup_inputs(seed: int = 0) -> dict:
    streams_of = jax.random.split(jax.random.key(seed), 7)
    u_band = noise(streams_of[0], (MROWS, K), 1.0, 6.0, ((0, 128),), jnp.float32)
    v_band = noise(streams_of[1], (MROWS, K), 1.0, 6.0, ((0, 128),), jnp.float32)
    y_left = noise(streams_of[2], (PANELS, MROWS, NB), MROWS ** -0.5, 0.046875, ((1, 128),), jnp.float32)
    t_left = noise(streams_of[3], (PANELS, NB, NB), 0.5, 3.0, (), jnp.float32)
    y_right = noise(streams_of[4], (PANELS, MROWS, NB), MROWS ** -0.5, 0.046875, ((1, 128),), jnp.float32)
    t_right = noise(streams_of[5], (PANELS, NB, NB), 0.5, 3.0, (), jnp.float32)
    return dict(u_band=u_band, v_band=v_band, y_left=y_left, t_left=t_left, y_right=y_right, t_right=t_right)


highest = lax.Precision.HIGHEST


def product(left, right):
    return jnp.dot(left, right, precision=highest, preferred_element_type=jnp.float32)


def apply_panels(matrix, reflectors_all, factors_all, transpose_factor):
    for panel in reversed(range(PANELS)):
        reflectors = reflectors_all[panel]
        factor = jnp.triu(factors_all[panel])
        if transpose_factor:
            factor = factor.T
        summed = product(reflectors.T, matrix)
        matrix = matrix - product(reflectors, product(factor, summed))
    return matrix


def reference(u_band, v_band, y_left, t_left, y_right, t_right):
    u_out = apply_panels(u_band, y_left, t_left, False)
    v_out = apply_panels(v_band, y_right, t_right, True)
    return u_out, v_out
```

```python
import functools

import jax
import jax.numpy as jnp
from jax import lax
from jax.experimental import pallas as pl
from jax.experimental.pallas import tpu as pltpu
from jax.sharding import PartitionSpec as P

MESH = pl.DeviceIdType.MESH
f32 = jnp.float32
bf16 = jnp.bfloat16
PAIRS = [(0, 1), (0, 2), (0, 3), (1, 2), (1, 3), (2, 3)]
VERT_OFFSETS = [(dx, dz, dc) for dx in (2, 1, 3, 0) for dz in (1, 0) for dc in (0, 1)][:-2] + [(0, 0, 1)]


def split(value):
    high = value.astype(bf16)
    return high, (value - high.astype(f32)).astype(bf16)


def dot(a, b):
    return lax.dot_general(a, b, (((1,), (0,)), ((), ())), preferred_element_type=f32)


def dot_t(a, b):
    return lax.dot_general(a, b, (((1,), (1,)), ((), ())), preferred_element_type=f32)


def three(a_high, a_low, b_high, b_low, product=dot):
    return product(a_high, b_high) + product(a_high, b_low) + product(a_low, b_high)


def exact(a, b):
    return jnp.dot(a, b, precision=lax.Precision.HIGHEST, preferred_element_type=f32)


def aligned(index, size):
    return pl.ds(pl.multiple_of(index * size, size), size)


def gram_kernel(yl, yr, out):
    for side, y in enumerate((yl, yr)):
        for place, (p, q) in enumerate(PAIRS):
            out[side * 6 + place] = exact(y[p].T, y[q])


def flat(offset):
    dx, dz, dc = offset
    return dx * 4 + dz * 2 + dc


def back(offset):
    dx, dz, dc = offset
    return ((4 - dx) % 4, dz, dc)


def move_kernel(
    yl, yr, u, v,
    u_out, v_out, yl_out, yr_out, sl_out, sr_out,
    ubuf, vbuf, ylbuf, yrbuf, ylt_h, ylt_l, yrt_h, yrt_l, acc,
    spr, core_in, x_in, shr, zl_in, sfr,
    spl, y_in, shl, zh_in, sfl,
    lsem, osem, yls, ylr, yrs, yrr, us, ur, vs, vr,
    rs, rr, ls, lr,
):
    a = lax.axis_index("au")
    t = lax.axis_index("vert")
    y, zh = a // 2, a % 2
    x, zl, c = t // 4, (t // 2) % 2, t % 2

    def vpos(dx, dz, dc):
        return lax.rem(x + dx, 4) * 4 + lax.rem(zl + dz, 2) * 2 + lax.rem(c + dc, 2)

    def apos(dy, dz):
        return lax.rem(y + dy, 4) * 2 + lax.rem(zh + dz, 2)

    sent = []

    def send(src, dst, ssem, rsem, device):
        copy = pltpu.make_async_remote_copy(
            src_ref=src, dst_ref=dst, send_sem=ssem, recv_sem=rsem,
            device_id=device, device_id_type=MESH,
        )
        copy.start()
        sent.append(copy)

    def arrive(dst, ssem, rsem):
        pltpu.make_async_remote_copy(
            src_ref=dst, dst_ref=dst, send_sem=ssem, recv_sem=rsem,
            device_id=(a, t), device_id_type=MESH,
        ).wait_recv()

    locals_y = []
    for p in range(4):
        locals_y.append(pltpu.make_async_copy(
            yl.at[p], ylbuf.at[aligned(t, 128), pl.ds(p * 128, 128)], lsem.at[p]))
        locals_y.append(pltpu.make_async_copy(
            yr.at[p], yrbuf.at[aligned(a, 128), pl.ds(p * 128, 128)], lsem.at[4 + p]))
    local_u = pltpu.make_async_copy(u.at[:, aligned(t, 512)], ubuf.at[aligned(t, 128), :], lsem.at[8])
    local_v = pltpu.make_async_copy(v.at[:, aligned(a, 1024)], vbuf.at[aligned(a, 128), :], lsem.at[9])
    for copy in locals_y + [local_u, local_v]:
        copy.start()

    barrier = pltpu.get_barrier_semaphore()
    for offset in VERT_OFFSETS:
        pl.semaphore_signal(barrier, inc=1, device_id=(a, vpos(*offset)), device_id_type=MESH)
    for o in range(1, 8):
        pl.semaphore_signal(barrier, inc=1, device_id=(apos(o // 2, o % 2), t), device_id_type=MESH)
    pl.semaphore_wait(barrier, 22)

    for copy in locals_y:
        copy.wait()

    def yl_slot(dx, dz, dc):
        return ylbuf.at[aligned(vpos(dx, dz, dc), 128), :]

    def yr_slot(dy, dz):
        return yrbuf.at[aligned(apos(dy, dz), 128), :]

    own = yl_slot(0, 0, 0)
    send(own, own, yls.at[0], ylr.at[2], (a, vpos(0, 1, 0)))
    for dx in (1, 2, 3):
        send(own, own, yls.at[dx], ylr.at[((4 - dx) % 4) * 4], (a, vpos(dx, 0, 0)))
    send(own, own, yls.at[7], ylr.at[1], (a, vpos(0, 0, 1)))
    mine = yr_slot(0, 0)
    send(mine, mine, yrs.at[0], yrr.at[1], (apos(0, 1), t))
    for dy in (1, 2, 3):
        send(mine, mine, yrs.at[dy], yrr.at[((4 - dy) % 4) * 2], (apos(dy, 0), t))

    for o in (5, 4, 3, 2, 7, 6, 1):
        dy, dz = o // 2, o % 2
        target = apos(dy, dz)
        send(v.at[:, aligned(target, 1024)], vbuf.at[aligned(a, 128), :],
             vs.at[o], vr.at[((4 - dy) % 4) * 2 + dz], (target, t))
    for part in range(2):
        for offset in VERT_OFFSETS:
            target = vpos(*offset)
            send(u.at[:, pl.ds(pl.multiple_of(target * 512 + part * 256, 256), 256)],
                 ubuf.at[aligned(t, 128), pl.ds(part * 256, 256)],
                 us.at[part, flat(offset)], ur.at[part, flat(back(offset))], (a, target))

    slot = yl_slot(0, 1, 0)
    arrive(slot, yls.at[0], ylr.at[2])
    for dx in (1, 2, 3):
        send(slot, slot, yls.at[3 + dx], ylr.at[((4 - dx) % 4) * 4 + 2], (a, vpos(dx, 0, 0)))
    send(slot, slot, yls.at[8], ylr.at[3], (a, vpos(0, 0, 1)))
    slot = yr_slot(0, 1)
    arrive(slot, yrs.at[0], yrr.at[1])
    for dy in (1, 2, 3):
        send(slot, slot, yrs.at[3 + dy], yrr.at[((4 - dy) % 4) * 2 + 1], (apos(dy, 0), t))
    for dz in (0, 1):
        for dx in (1, 2, 3):
            slot = yl_slot(dx, dz, 0)
            arrive(slot, yls.at[0], ylr.at[dx * 4 + dz * 2])
            send(slot, slot, yls.at[8 + dz * 3 + dx], ylr.at[dx * 4 + dz * 2 + 1], (a, vpos(0, 0, 1)))
    for dz in (0, 1):
        for dy in (1, 2, 3):
            arrive(yr_slot(dy, dz), yrs.at[0], yrr.at[dy * 2 + dz])

    def turn(source, high, low, count):
        def body(j, carry):
            high_part, low_part = split(source[aligned(j, 128), :].T)
            high[:, aligned(j, 128)] = high_part
            low[:, aligned(j, 128)] = low_part
            return carry
        lax.fori_loop(0, count, body, 0)

    turn(yrbuf, yrt_h, yrt_l, 8)

    local_v.wait()
    for o in range(1, 8):
        arrive(vbuf.at[aligned(apos(o // 2, o % 2), 128), :], vs.at[o], vr.at[o])
    out_copies = [
        pltpu.make_async_copy(vbuf, v_out, osem.at[0]),
        pltpu.make_async_copy(yrbuf, yr_out, osem.at[1]),
    ]
    for copy in out_copies:
        copy.start()

    def right_tile(n, carry):
        acc[...] = jnp.zeros_like(acc)

        def step(k, carry):
            high, low = split(vbuf[aligned(k, 512), aligned(n, 256)])
            acc[...] += three(yrt_h[:, aligned(k, 512)], yrt_l[:, aligned(k, 512)], high, low)
            return carry
        lax.fori_loop(0, 2, step, 0)
        spr[aligned(n, 256), :] = acc[...].T
        return carry
    lax.fori_loop(0, 4, right_tile, 0)

    send(spr.at[aligned(1 - c, 512), :], core_in, rs.at[0], rr.at[0], (a, vpos(0, 0, 1)))

    for o in range(1, 16, 2):
        arrive(yl_slot(o // 4, (o // 2) % 2, 1), yls.at[0], ylr.at[o])
    copy = pltpu.make_async_copy(ylbuf, yl_out, osem.at[2])
    copy.start()
    out_copies.append(copy)
    turn(ylbuf, ylt_h, ylt_l, 16)

    arrive(core_in, rs.at[0], rr.at[0])
    spr[aligned(c, 512), :] += core_in[...]
    for dx in (2, 1, 3):
        send(spr.at[aligned(c * 4 + lax.rem(x + dx, 4), 128), :], x_in.at[(4 - dx) % 4 - 1],
             rs.at[dx], rr.at[(4 - dx) % 4], (a, vpos(dx, 0, 0)))
    for dx in (1, 2, 3):
        arrive(x_in.at[dx - 1], rs.at[dx], rr.at[dx])
    place = aligned(c * 4 + x, 128)
    shr[...] = spr[place, :] + x_in[0] + x_in[1] + x_in[2]
    send(shr, zl_in, rs.at[4], rr.at[4], (a, vpos(0, 1, 0)))
    arrive(zl_in, rs.at[4], rr.at[4])
    sfr[place, :] = shr[...] + zl_in[...]
    for dx in (2, 1, 3):
        send(sfr.at[place, :], sfr.at[place, :], rs.at[4 + dx], rr.at[4 + (4 - dx) % 4], (a, vpos(dx, 0, 0)))
    send(sfr.at[place, :], sfr.at[place, :], rs.at[8], rr.at[8], (a, vpos(0, 0, 1)))

    local_u.wait()

    def left_part(part):
        for offset in VERT_OFFSETS:
            arrive(ubuf.at[aligned(vpos(*offset), 128), pl.ds(part * 256, 256)],
                   us.at[part, flat(offset)], ur.at[part, flat(offset)])
        copy = pltpu.make_async_copy(
            ubuf.at[:, pl.ds(part * 256, 256)], u_out.at[:, pl.ds(part * 256, 256)], osem.at[3 + part])
        copy.start()
        out_copies.append(copy)
        acc[...] = jnp.zeros_like(acc)

        def step(k, carry):
            high, low = split(ubuf[aligned(k, 512), pl.ds(part * 256, 256)])
            acc[...] += three(ylt_h[:, aligned(k, 512)], ylt_l[:, aligned(k, 512)], high, low)
            return carry
        lax.fori_loop(0, 4, step, 0)
        spl[part] = acc[...].T
        for dy in (2, 1, 3):
            send(spl.at[part, aligned(lax.rem(y + dy, 4), 64), :], y_in.at[part, (4 - dy) % 4 - 1],
                 ls.at[part, dy], lr.at[part, (4 - dy) % 4], (apos(dy, 0), t))

    def left_reduce(part):
        for dy in (1, 2, 3):
            arrive(y_in.at[part, dy - 1], ls.at[part, dy], lr.at[part, dy])
        shl[part] = spl[part, aligned(y, 64), :] + y_in[part, 0] + y_in[part, 1] + y_in[part, 2]
        send(shl.at[part], zh_in.at[part], ls.at[part, 4], lr.at[part, 4], (apos(0, 1), t))
        arrive(zh_in.at[part], ls.at[part, 4], lr.at[part, 4])
        spot = aligned(part * 4 + y, 64)
        sfl[spot, :] = shl[part] + zh_in[part]
        for dy in (2, 1, 3):
            send(sfl.at[spot, :], sfl.at[spot, :], ls.at[part, 4 + dy], lr.at[part, 4 + (4 - dy) % 4],
                 (apos(dy, 0), t))

    left_part(0)

    for dx in (1, 2, 3):
        got = sfr.at[aligned(c * 4 + lax.rem(x + dx, 4), 128), :]
        arrive(got, rs.at[0], rr.at[4 + dx])
        send(got, got, rs.at[8 + dx], rr.at[8 + dx], (a, vpos(0, 0, 1)))

    left_reduce(0)

    for dx in (0, 1, 2, 3):
        arrive(sfr.at[aligned((1 - c) * 4 + lax.rem(x + dx, 4), 128), :], rs.at[0], rr.at[8 + dx])
    copy = pltpu.make_async_copy(sfr, sr_out, osem.at[5])
    copy.start()
    out_copies.append(copy)

    left_part(1)
    left_reduce(1)
    for part in range(2):
        for dy in (1, 2, 3):
            arrive(sfl.at[aligned(part * 4 + lax.rem(y + dy, 4), 64), :], ls.at[part, dy], lr.at[part, 4 + dy])
    copy = pltpu.make_async_copy(sfl, sl_out, osem.at[6])
    copy.start()
    out_copies.append(copy)
    for copy in sent:
        copy.wait_send()
    for copy in out_copies:
        copy.wait()


def merged(factors, grams):
    rows = [None] * 4
    for p in (3, 2, 1, 0):
        unit = (lax.broadcasted_iota(jnp.int32, (128, 512), 0) + p * 128
                == lax.broadcasted_iota(jnp.int32, (128, 512), 1)).astype(f32)
        for q in range(p + 1, 4):
            unit = unit - exact(grams[PAIRS.index((p, q))], rows[q])
        rows[p] = exact(factors[p], unit)
    return jnp.concatenate(rows, axis=0)


def update_kernel(tl, tr, grams, sl, sr, yl, u, yr, v, u_out, v_out, wl_h, wl_l, wr_h, wr_l):
    step = pl.program_id(0)
    upper = (lax.broadcasted_iota(jnp.int32, (128, 128), 0)
             <= lax.broadcasted_iota(jnp.int32, (128, 128), 1))

    @pl.when(step == 0)
    def _():
        factors = [jnp.where(upper, tl[p], 0.0) for p in range(4)]
        total = merged(factors, [grams[i] for i in range(6)])
        high, low = split(total)
        s_high, s_low = split(sl[...])
        wl_h[...], wl_l[...] = split(three(high, low, s_high, s_low, dot_t))
        factors = [jnp.where(upper, tr[p], 0.0).T for p in range(4)]
        total = merged(factors, [grams[6 + i] for i in range(6)])
        high, low = split(total)
        s_high, s_low = split(sr[...])
        wr_h[...], wr_l[...] = split(three(high, low, s_high, s_low, dot_t))

    @pl.when(step < 4)
    def _():
        high, low = split(yl[...])
        u_out[...] = u[...] - three(high, low, wl_h[...], wl_l[...])

    @pl.when(step >= 4)
    def _():
        high, low = split(yr[...])
        v_out[...] = v[...] - three(high, low, wr_h[...], wr_l[...])


def shards(u_band, v_band, y_left, t_left, y_right, t_right):
    any_space = pl.BlockSpec(memory_space=pl.ANY)
    vmem = pl.BlockSpec(memory_space=pltpu.VMEM)
    shape = jax.ShapeDtypeStruct
    grams = pl.pallas_call(
        gram_kernel,
        out_shape=shape((12, 128, 128), f32),
        in_specs=[vmem, vmem],
        out_specs=vmem,
    )(y_left, y_right)
    grams = lax.psum(grams, ("au", "vert"))

    dma = pltpu.SemaphoreType.DMA
    buf = lambda *dims: pltpu.VMEM(dims, f32)
    half = lambda *dims: pltpu.VMEM(dims, bf16)
    u_all, v_all, yl_all, yr_all, s_left, s_right = pl.pallas_call(
        move_kernel,
        out_shape=[
            shape((2048, 512), f32), shape((1024, 1024), f32),
            shape((2048, 512), f32), shape((1024, 512), f32),
            shape((512, 512), f32), shape((1024, 512), f32),
        ],
        in_specs=[any_space] * 4,
        out_specs=[any_space] * 6,
        scratch_shapes=[
            buf(2048, 512), buf(1024, 1024), buf(2048, 512), buf(1024, 512),
            half(512, 2048), half(512, 2048), half(512, 1024), half(512, 1024), buf(512, 256),
            buf(1024, 512), buf(512, 512), buf(3, 128, 512), buf(128, 512), buf(128, 512), buf(1024, 512),
            buf(2, 256, 512), buf(2, 3, 64, 512), buf(2, 64, 512), buf(2, 64, 512), buf(512, 512),
            dma((10,)), dma((8,)), dma((16,)), dma((16,)), dma((8,)), dma((8,)),
            dma((2, 16)), dma((2, 16)), dma((8,)), dma((8,)),
            dma((12,)), dma((12,)), dma((2, 8)), dma((2, 8)),
        ],
        compiler_params=pltpu.CompilerParams(
            collective_id=0, has_side_effects=True, vmem_limit_bytes=48 * 2**20,
        ),
        cost_estimate=pl.CostEstimate(flops=2 * 10**10, bytes_accessed=4 * 10**8, transcendentals=0),
    )(y_left, y_right, u_band, v_band)

    first = lambda i: (jnp.minimum(i, 3), 0)
    second = lambda i: (jnp.maximum(i - 4, 0), 0)
    whole2 = lambda i: (0, 0)
    whole3 = lambda i: (0, 0, 0)
    return pl.pallas_call(
        update_kernel,
        grid=(8,),
        out_shape=[shape((2048, 512), f32), shape((1024, 1024), f32)],
        in_specs=[
            pl.BlockSpec((4, 128, 128), whole3), pl.BlockSpec((4, 128, 128), whole3),
            pl.BlockSpec((12, 128, 128), whole3),
            pl.BlockSpec((512, 512), whole2), pl.BlockSpec((1024, 512), whole2),
            pl.BlockSpec((512, 512), first), pl.BlockSpec((512, 512), first),
            pl.BlockSpec((256, 512), second), pl.BlockSpec((256, 1024), second),
        ],
        out_specs=[pl.BlockSpec((512, 512), first), pl.BlockSpec((256, 1024), second)],
        scratch_shapes=[half(512, 512), half(512, 512), half(512, 1024), half(512, 1024)],
        compiler_params=pltpu.CompilerParams(vmem_limit_bytes=48 * 2**20),
    )(t_left, t_right, grams, s_left, s_right, yl_all, u_all, yr_all, v_all)


def solution(mesh):
    return jax.shard_map(
        shards,
        mesh=mesh,
        in_specs=(
            P(("au", "vert"), None),
            P(("vert", "au"), None),
            P(None, ("au", "vert"), None),
            P(),
            P(None, ("vert", "au"), None),
            P(),
        ),
        out_specs=(P("au", "vert"), P("vert", "au")),
        check_vma=False,
    )
```

```python
import functools

import jax
import jax.numpy as jnp
from jax import lax
from jax.experimental import pallas as pl
from jax.experimental.pallas import tpu as pltpu
from jax.sharding import PartitionSpec as P

MESH = pl.DeviceIdType.MESH
f32 = jnp.float32
bf16 = jnp.bfloat16
PARTS = (256, 256)
STARTS = [sum(PARTS[:part]) for part in range(len(PARTS))]
PAIRS = [(0, 1), (0, 2), (0, 3), (1, 2), (1, 3), (2, 3)]
VERT_OFFSETS = [(dx, dz, dc) for dx in (2, 1, 3, 0) for dz in (1, 0) for dc in (0, 1)][:-2] + [(0, 0, 1)]


def split(value):
    high = value.astype(bf16)
    return high, (value - high.astype(f32)).astype(bf16)


def dot(a, b):
    return lax.dot_general(a, b, (((1,), (0,)), ((), ())), preferred_element_type=f32)


def dot_t(a, b):
    return lax.dot_general(a, b, (((1,), (1,)), ((), ())), preferred_element_type=f32)


def three(a_high, a_low, b_high, b_low, product=dot):
    return product(a_high, b_high) + product(a_high, b_low) + product(a_low, b_high)


def exact(a, b):
    return jnp.dot(a, b, precision=lax.Precision.HIGHEST, preferred_element_type=f32)


def aligned(index, size):
    return pl.ds(pl.multiple_of(index * size, size), size)


def flat(offset):
    dx, dz, dc = offset
    return dx * 4 + dz * 2 + dc


def back(offset):
    dx, dz, dc = offset
    return ((4 - dx) % 4, dz, dc)


def merged(factors, grams):
    rows = [None] * 4
    for p in (3, 2, 1, 0):
        unit = (lax.broadcasted_iota(jnp.int32, (128, 512), 0) + p * 128
                == lax.broadcasted_iota(jnp.int32, (128, 512), 1)).astype(f32)
        for q in range(p + 1, 4):
            unit = unit - exact(grams[PAIRS.index((p, q))], rows[q])
        rows[p] = exact(factors[p], unit)
    return jnp.concatenate(rows, axis=0)


def upper(t):
    keep = (lax.broadcasted_iota(jnp.int32, (128, 128), 0)
            <= lax.broadcasted_iota(jnp.int32, (128, 128), 1))
    return jnp.where(keep, t, 0.0)


def move_kernel(
    yl, yr, u, v, tl_in, tr_in,
    u_out, v_out, yl_out, yr_out, wl_out, wr_out,
    ubuf, vbuf, ylbuf, yrbuf, ylt_h, ylt_l, yrt_h, yrt_l,
    spr, core_in, x_in, shr, zl_in, wr,
    spl, y_in, shl, zh_in, wl,
    gl, gl_in, gl_sh, gl_z, gl_all, gr, gr_core, gr_sum, gr_in, gr_sh, gr_z, gr_all,
    tl_h, tl_l, tr_h, tr_l, tl, tr,
    lsem, osem, yls, ylr, yrs, yrr, us, ur, vs, vr,
    rs, rr, ls, lr, gls, glr, grs, grr,
):
    a = lax.axis_index("au")
    t = lax.axis_index("vert")
    y, zh = a // 2, a % 2
    x, zl, c = t // 4, (t // 2) % 2, t % 2

    def vpos(dx, dz, dc):
        return lax.rem(x + dx, 4) * 4 + lax.rem(zl + dz, 2) * 2 + lax.rem(c + dc, 2)

    def apos(dy, dz):
        return lax.rem(y + dy, 4) * 2 + lax.rem(zh + dz, 2)

    sent = []

    def send(src, dst, ssem, rsem, device):
        copy = pltpu.make_async_remote_copy(
            src_ref=src, dst_ref=dst, send_sem=ssem, recv_sem=rsem,
            device_id=device, device_id_type=MESH,
        )
        copy.start()
        sent.append(copy)

    def arrive(dst, sem):
        pltpu.make_async_remote_copy(
            src_ref=dst, dst_ref=dst, send_sem=sem, recv_sem=sem,
            device_id=(a, t), device_id_type=MESH,
        ).wait_recv()

    out_copies = []

    def put(src, dst, sem):
        copy = pltpu.make_async_copy(src, dst, sem)
        copy.start()
        out_copies.append(copy)

    locals_y = []
    for p in range(4):
        locals_y.append(pltpu.make_async_copy(
            yl.at[p], ylbuf.at[aligned(t, 128), pl.ds(p * 128, 128)], lsem.at[p]))
        locals_y.append(pltpu.make_async_copy(
            yr.at[p], yrbuf.at[aligned(a, 128), pl.ds(p * 128, 128)], lsem.at[4 + p]))
    local_u = pltpu.make_async_copy(u.at[:, aligned(t, 512)], ubuf.at[aligned(t, 128), :], lsem.at[8])
    local_v = pltpu.make_async_copy(v.at[:, aligned(a, 1024)], vbuf.at[aligned(a, 128), :], lsem.at[9])
    local_t = [pltpu.make_async_copy(tl_in, tl, lsem.at[10]), pltpu.make_async_copy(tr_in, tr, lsem.at[11])]
    for copy in locals_y + [local_u, local_v] + local_t:
        copy.start()

    barrier = pltpu.get_barrier_semaphore()
    for offset in VERT_OFFSETS:
        pl.semaphore_signal(barrier, inc=1, device_id=(a, vpos(*offset)), device_id_type=MESH)
    for o in range(1, 8):
        pl.semaphore_signal(barrier, inc=1, device_id=(apos(o // 2, o % 2), t), device_id_type=MESH)
    pl.semaphore_wait(barrier, 22)

    for copy in locals_y:
        copy.wait()

    def yl_slot(dx, dz, dc):
        return ylbuf.at[aligned(vpos(dx, dz, dc), 128), :]

    def yr_slot(dy, dz):
        return yrbuf.at[aligned(apos(dy, dz), 128), :]

    def send_v(part, o):
        dy, dz = o // 2, o % 2
        target = apos(dy, dz)
        begin, width = 2 * STARTS[part], 2 * PARTS[part]
        send(v.at[:, pl.ds(pl.multiple_of(target * 1024 + begin, 256), width)],
             vbuf.at[aligned(a, 128), pl.ds(begin, width)],
             vs.at[part, o], vr.at[part, ((4 - dy) % 4) * 2 + dz], (target, t))

    def send_u(part, offset):
        target = vpos(*offset)
        begin, width = STARTS[part], PARTS[part]
        send(u.at[:, pl.ds(pl.multiple_of(target * 512 + begin, 128), width)],
             ubuf.at[aligned(t, 128), pl.ds(begin, width)],
             us.at[part, flat(offset)], ur.at[part, flat(back(offset))], (a, target))

    def in_plane(part):
        for o in (2, 6, 4):
            send_v(part, o)
        for dc in (0, 1):
            for dx in (1, 3, 2):
                send_u(part, (dx, 0, dc))
        send_u(part, (0, 0, 1))

    def across(part):
        for o, dx in ((1, 0), (3, 1), (7, 3), (5, 2)):
            send_v(part, o)
            for dc in (0, 1):
                send_u(part, (dx, 1, dc))

    own = yl_slot(0, 0, 0)
    mine = yr_slot(0, 0)
    send(own, own, yls.at[0], ylr.at[2], (a, vpos(0, 1, 0)))
    send(mine, mine, yrs.at[0], yrr.at[1], (apos(0, 1), t))
    for d in (1, 3, 2):
        send(own, own, yls.at[d], ylr.at[((4 - d) % 4) * 4], (a, vpos(d, 0, 0)))
        send(mine, mine, yrs.at[d], yrr.at[((4 - d) % 4) * 2], (apos(d, 0), t))
    send(own, own, yls.at[7], ylr.at[1], (a, vpos(0, 0, 1)))

    slot = yl_slot(0, 1, 0)
    arrive(slot, ylr.at[2])
    for dx in (1, 3, 2):
        send(slot, slot, yls.at[3 + dx], ylr.at[((4 - dx) % 4) * 4 + 2], (a, vpos(dx, 0, 0)))
    send(slot, slot, yls.at[8], ylr.at[3], (a, vpos(0, 0, 1)))
    slot = yr_slot(0, 1)
    arrive(slot, yrr.at[1])
    for dy in (1, 3, 2):
        send(slot, slot, yrs.at[3 + dy], yrr.at[((4 - dy) % 4) * 2 + 1], (apos(dy, 0), t))

    across(0)
    in_plane(0)
    for dz in (0, 1):
        for dx in (1, 3, 2):
            slot = yl_slot(dx, dz, 0)
            arrive(slot, ylr.at[dx * 4 + dz * 2])
            send(slot, slot, yls.at[8 + dz * 3 + dx], ylr.at[dx * 4 + dz * 2 + 1], (a, vpos(0, 0, 1)))

    def turn(source, high, low, count):
        def body(j, carry):
            high_part, low_part = split(source[aligned(j, 128), :].T)
            high[:, aligned(j, 128)] = high_part
            low[:, aligned(j, 128)] = low_part
            return carry
        lax.fori_loop(0, count, body, 0)

    def gram(high, low, out):
        def block(p, n, q, m):
            rows, cols = pl.ds(p * 128, n * 128), pl.ds(q * 128, m * 128)
            return three(high[rows, :], low[rows, :], high[cols, :], low[cols, :], dot_t)
        out[0:128, :] = block(0, 1, 1, 1)
        square = block(0, 2, 2, 2)
        out[128:256, :] = square[:128, :128]
        out[256:384, :] = square[:128, 128:]
        out[384:512, :] = square[128:, :128]
        out[512:640, :] = square[128:, 128:]
        out[640:768, :] = block(2, 1, 3, 1)

    def gram_left():
        for dy in (1, 3, 2):
            send(gl.at[aligned(lax.rem(y + dy, 4), 192), :], gl_in.at[(4 - dy) % 4 - 1],
                 gls.at[dy], glr.at[(4 - dy) % 4], (apos(dy, 0), t))

    def gram_right():
        arrive(gr_core, grr.at[0])
        gr_sum[...] = gr[...] + gr_core[...]
        for dx in (1, 3, 2):
            send(gr_sum.at[aligned(lax.rem(x + dx, 4), 192), :], gr_in.at[(4 - dx) % 4 - 1],
                 grs.at[dx], grr.at[(4 - dx) % 4], (a, vpos(dx, 0, 0)))

    def gram_pair_left():
        for dy in (1, 3, 2):
            arrive(gl_in.at[dy - 1], glr.at[dy])
        gl_sh[...] = gl[aligned(y, 192), :] + gl_in[0] + gl_in[1] + gl_in[2]
        send(gl_sh, gl_z, gls.at[4], glr.at[4], (apos(0, 1), t))

    def gram_pair_right():
        for dx in (1, 3, 2):
            arrive(gr_in.at[dx - 1], grr.at[dx])
        gr_sh[...] = gr_sum[aligned(x, 192), :] + gr_in[0] + gr_in[1] + gr_in[2]
        send(gr_sh, gr_z, grs.at[4], grr.at[4], (a, vpos(0, 1, 0)))

    def gram_spread_left():
        arrive(gl_z, glr.at[4])
        spot_l = gl_all.at[aligned(y, 192), :]
        spot_l[...] = gl_sh[...] + gl_z[...]
        for dy in (1, 3, 2):
            send(spot_l, spot_l, gls.at[4 + dy], glr.at[4 + (4 - dy) % 4], (apos(dy, 0), t))

    def gram_spread_right():
        arrive(gr_z, grr.at[4])
        spot_r = gr_all.at[aligned(x, 192), :]
        spot_r[...] = gr_sh[...] + gr_z[...]
        for dx in (1, 3, 2):
            send(spot_r, spot_r, grs.at[4 + dx], grr.at[4 + (4 - dx) % 4], (a, vpos(dx, 0, 0)))

    def merge_left():
        for dy in (1, 2, 3):
            arrive(gl_all.at[aligned(lax.rem(y + dy, 4), 192), :], glr.at[4 + dy])
        tl_h[...], tl_l[...] = split(merged(
            [upper(tl[p]) for p in range(4)], [gl_all[pl.ds(i * 128, 128), :] for i in range(6)]))

    def merge_right():
        for dx in (1, 2, 3):
            arrive(gr_all.at[aligned(lax.rem(x + dx, 4), 192), :], grr.at[4 + dx])
        tr_h[...], tr_l[...] = split(merged(
            [upper(tr[p]).T for p in range(4)], [gr_all[pl.ds(i * 128, 128), :] for i in range(6)]))

    for o in range(1, 16, 2):
        arrive(yl_slot(o // 4, (o // 2) % 2, 1), ylr.at[o])
    put(ylbuf, yl_out, osem.at[1])
    turn(ylbuf, ylt_h, ylt_l, 16)
    gram(ylt_h, ylt_l, gl)
    gram_left()

    for dz in (0, 1):
        for dy in (1, 3, 2):
            arrive(yr_slot(dy, dz), yrr.at[dy * 2 + dz])
    put(yrbuf, yr_out, osem.at[0])
    turn(yrbuf, yrt_h, yrt_l, 8)
    gram(yrt_h, yrt_l, gr)
    send(gr, gr_core, grs.at[0], grr.at[0], (a, vpos(0, 0, 1)))

    gram_right()
    across(1)
    in_plane(1)
    for copy in local_t + [local_u, local_v]:
        copy.wait()
    def right_sums(part):
        begin, width = 2 * STARTS[part], 2 * PARTS[part]
        for o in range(1, 8):
            arrive(vbuf.at[aligned(apos(o // 2, o % 2), 128), pl.ds(begin, width)], vr.at[part, o])
        put(vbuf.at[:, pl.ds(begin, width)], v_out.at[:, pl.ds(begin, width)], osem.at[2 + part])

        def tile(n, carry):
            columns = pl.ds(pl.multiple_of(begin + n * 256, 256), 256)
            high, low = split(vbuf[:, columns])
            spr[columns, :] = three(yrt_h[...], yrt_l[...], high, low).T
            return carry
        lax.fori_loop(0, width // 256, tile, 0)
        half = PARTS[part]
        send(spr.at[pl.ds(pl.multiple_of(begin + (1 - c) * half, 128), half), :],
             core_in.at[pl.ds(STARTS[part], half), :], rs.at[part, 0], rr.at[part, 0], (a, vpos(0, 0, 1)))

    def right_share(part, core, row):
        half = PARTS[part]
        return pl.ds(pl.multiple_of(2 * STARTS[part] + core * half + row * (half // 4), 32), half // 4)

    def left_share(part, row):
        quarter = PARTS[part] // 4
        return pl.ds(pl.multiple_of(STARTS[part] + row * quarter, 32), quarter)

    def inner(part):
        return pl.ds(STARTS[part] // 4, PARTS[part] // 4)

    def right_core(part):
        half = PARTS[part]
        arrive(core_in.at[pl.ds(STARTS[part], half), :], rr.at[part, 0])
        mine = pl.ds(pl.multiple_of(2 * STARTS[part] + c * half, 128), half)
        spr[mine, :] += core_in[pl.ds(STARTS[part], half), :]
        for dx in (1, 3, 2):
            send(spr.at[right_share(part, c, lax.rem(x + dx, 4)), :], x_in.at[(4 - dx) % 4 - 1, inner(part), :],
                 rs.at[part, dx], rr.at[part, (4 - dx) % 4], (a, vpos(dx, 0, 0)))

    def right_pair(part):
        for dx in (1, 2, 3):
            arrive(x_in.at[dx - 1, inner(part), :], rr.at[part, dx])
        at = inner(part)
        shr[at, :] = spr[right_share(part, c, x), :] + x_in[0, at, :] + x_in[1, at, :] + x_in[2, at, :]
        send(shr.at[at, :], zl_in.at[at, :], rs.at[part, 4], rr.at[part, 4], (a, vpos(0, 1, 0)))

    def right_spread(part):
        at = inner(part)
        arrive(zl_in.at[at, :], rr.at[part, 4])
        high, low = split(shr[at, :] + zl_in[at, :])
        place = wr.at[right_share(part, c, x), :]
        place[...] = three(high, low, tr_h[...], tr_l[...], dot_t)
        for dx in (1, 3, 2):
            send(place, place, rs.at[part, 4 + dx], rr.at[part, 4 + (4 - dx) % 4], (a, vpos(dx, 0, 0)))
        send(place, place, rs.at[part, 8], rr.at[part, 8], (a, vpos(0, 0, 1)))

    def right_onward(part):
        for dx in (1, 3, 2):
            got = wr.at[right_share(part, c, lax.rem(x + dx, 4)), :]
            arrive(got, rr.at[part, 4 + dx])
            send(got, got, rs.at[part, 8 + dx], rr.at[part, 8 + dx], (a, vpos(0, 0, 1)))

    def right_done(part):
        for dx in (0, 1, 2, 3):
            arrive(wr.at[right_share(part, 1 - c, lax.rem(x + dx, 4)), :], rr.at[part, 8 + dx])

    def left_sums(part):
        begin, width = STARTS[part], PARTS[part]
        for offset in VERT_OFFSETS:
            arrive(ubuf.at[aligned(vpos(*offset), 128), pl.ds(begin, width)], ur.at[part, flat(offset)])
        put(ubuf.at[:, pl.ds(begin, width)], u_out.at[:, pl.ds(begin, width)], osem.at[4 + part])
        for tile in range(begin, begin + width, 256):
            columns = pl.ds(tile, min(256, begin + width - tile))
            high, low = split(ubuf[:, columns])
            spl[columns, :] = three(ylt_h[...], ylt_l[...], high, low).T
        for dy in (1, 3, 2):
            send(spl.at[left_share(part, lax.rem(y + dy, 4)), :], y_in.at[(4 - dy) % 4 - 1, inner(part), :],
                 ls.at[part, dy], lr.at[part, (4 - dy) % 4], (apos(dy, 0), t))

    def left_pair(part):
        at = inner(part)
        for dy in (1, 2, 3):
            arrive(y_in.at[dy - 1, at, :], lr.at[part, dy])
        shl[at, :] = spl[left_share(part, y), :] + y_in[0, at, :] + y_in[1, at, :] + y_in[2, at, :]
        send(shl.at[at, :], zh_in.at[at, :], ls.at[part, 4], lr.at[part, 4], (apos(0, 1), t))

    def left_spread(part):
        at = inner(part)
        arrive(zh_in.at[at, :], lr.at[part, 4])
        high, low = split(shl[at, :] + zh_in[at, :])
        place = wl.at[left_share(part, y), :]
        place[...] = three(high, low, tl_h[...], tl_l[...], dot_t)
        for dy in (1, 3, 2):
            send(place, place, ls.at[part, 4 + dy], lr.at[part, 4 + (4 - dy) % 4], (apos(dy, 0), t))

    def left_done(part):
        for dy in (1, 2, 3):
            arrive(wl.at[left_share(part, lax.rem(y + dy, 4)), :], lr.at[part, 4 + dy])

    right_sums(0)
    left_sums(0)
    right_core(0)
    gram_pair_right()
    gram_pair_left()
    left_pair(0)
    right_pair(0)
    gram_spread_right()
    gram_spread_left()
    right_sums(1)
    left_sums(1)
    right_core(1)
    merge_right()
    merge_left()
    left_spread(0)
    right_spread(0)
    left_pair(1)
    right_pair(1)
    right_onward(0)
    left_spread(1)
    right_spread(1)
    right_onward(1)
    for part in range(2):
        left_done(part)
        right_done(part)
    put(wr, wr_out, osem.at[6])
    put(wl, wl_out, osem.at[7])
    for copy in sent:
        copy.wait_send()
    for copy in out_copies:
        copy.wait()


def update_kernel(wl, yl, u, yr, v, wr, u_out, v_out, wl_h, wl_l, wr_h, wr_l):
    step = pl.program_id(0)

    @pl.when(step == 0)
    def _():
        wl_h[...], wl_l[...] = split(wl[...])

    @pl.when(step == 4)
    def _():
        wr_h[...], wr_l[...] = split(wr[...])

    @pl.when(step < 4)
    def _():
        high, low = split(yl[...])
        u_out[...] = u[...] - three(high, low, wl_h[...], wl_l[...], dot_t)

    @pl.when(step >= 4)
    def _():
        high, low = split(yr[...])
        v_out[...] = v[...] - three(high, low, wr_h[...], wr_l[...], dot_t)


def shards(u_band, v_band, y_left, t_left, y_right, t_right):
    any_space = pl.BlockSpec(memory_space=pl.ANY)
    shape = jax.ShapeDtypeStruct
    dma = pltpu.SemaphoreType.DMA
    buf = lambda *dims: pltpu.VMEM(dims, f32)
    half = lambda *dims: pltpu.VMEM(dims, bf16)
    u_all, v_all, yl_all, yr_all, w_left, w_right = pl.pallas_call(
        move_kernel,
        out_shape=[
            shape((2048, 512), f32), shape((1024, 1024), f32),
            shape((2048, 512), f32), shape((1024, 512), f32),
            shape((512, 512), f32), shape((1024, 512), f32),
        ],
        in_specs=[any_space] * 6,
        out_specs=[any_space] * 6,
        scratch_shapes=[
            buf(2048, 512), buf(1024, 1024), buf(2048, 512), buf(1024, 512),
            half(512, 2048), half(512, 2048), half(512, 1024), half(512, 1024),
            buf(1024, 512), buf(512, 512), buf(3, 128, 512), buf(128, 512), buf(128, 512), buf(1024, 512),
            buf(512, 512), buf(3, 128, 512), buf(128, 512), buf(128, 512), buf(512, 512),
            buf(768, 128), buf(3, 192, 128), buf(192, 128), buf(192, 128), buf(768, 128),
            buf(768, 128), buf(768, 128), buf(768, 128), buf(3, 192, 128), buf(192, 128), buf(192, 128), buf(768, 128),
            half(512, 512), half(512, 512), half(512, 512), half(512, 512),
            buf(4, 128, 128), buf(4, 128, 128),
            dma((12,)), dma((8,)), dma((16,)), dma((16,)), dma((8,)), dma((8,)),
            dma((len(PARTS), 16)), dma((len(PARTS), 16)), dma((len(PARTS), 8)), dma((len(PARTS), 8)),
            dma((len(PARTS), 12)), dma((len(PARTS), 12)), dma((len(PARTS), 8)), dma((len(PARTS), 8)),
            dma((8,)), dma((8,)), dma((8,)), dma((8,)),
        ],
        compiler_params=pltpu.CompilerParams(
            collective_id=0, has_side_effects=True, vmem_limit_bytes=60 * 2**20,
        ),
        cost_estimate=pl.CostEstimate(flops=2 * 10**10, bytes_accessed=4 * 10**8, transcendentals=0),
    )(y_left, y_right, u_band, v_band, t_left, t_right)

    first = lambda i: (jnp.minimum(i, 3), 0)
    second = lambda i: (jnp.maximum(i - 4, 0), 0)
    whole = lambda i: (0, 0)
    return pl.pallas_call(
        update_kernel,
        grid=(8,),
        out_shape=[shape((2048, 512), f32), shape((1024, 1024), f32)],
        in_specs=[
            pl.BlockSpec((512, 512), whole),
            pl.BlockSpec((512, 512), first), pl.BlockSpec((512, 512), first),
            pl.BlockSpec((256, 512), second), pl.BlockSpec((256, 1024), second),
            pl.BlockSpec((1024, 512), whole),
        ],
        out_specs=[pl.BlockSpec((512, 512), first), pl.BlockSpec((256, 1024), second)],
        scratch_shapes=[half(512, 512), half(512, 512), half(1024, 512), half(1024, 512)],
        compiler_params=pltpu.CompilerParams(vmem_limit_bytes=48 * 2**20),
    )(w_left, yl_all, u_all, yr_all, v_all, w_right)


def solution(mesh):
    return jax.shard_map(
        shards,
        mesh=mesh,
        in_specs=(
            P(("au", "vert"), None),
            P(("vert", "au"), None),
            P(None, ("au", "vert"), None),
            P(),
            P(None, ("vert", "au"), None),
            P(),
        ),
        out_specs=(P("au", "vert"), P("vert", "au")),
        check_vma=False,
    )
```

```python
import functools

import jax
import jax.numpy as jnp
from jax import lax
from jax.experimental import pallas as pl
from jax.experimental.pallas import tpu as pltpu
from jax.sharding import PartitionSpec as P

MESH = pl.DeviceIdType.MESH
f32 = jnp.float32
bf16 = jnp.bfloat16
PARTS = (256, 256)
STARTS = [sum(PARTS[:part]) for part in range(len(PARTS))]
PAIRS = [(0, 1), (0, 2), (0, 3), (1, 2), (1, 3), (2, 3)]
VERT_OFFSETS = [(dx, dz, dc) for dx in (2, 1, 3, 0) for dz in (1, 0) for dc in (0, 1)][:-2] + [(0, 0, 1)]


def split(value):
    high = value.astype(bf16)
    return high, (value - high.astype(f32)).astype(bf16)


def dot(a, b):
    return lax.dot_general(a, b, (((1,), (0,)), ((), ())), preferred_element_type=f32)


def dot_t(a, b):
    return lax.dot_general(a, b, (((1,), (1,)), ((), ())), preferred_element_type=f32)


def three(a_high, a_low, b_high, b_low, product=dot):
    return product(a_high, b_high) + product(a_high, b_low) + product(a_low, b_high)


def exact(a, b):
    return jnp.dot(a, b, precision=lax.Precision.HIGHEST, preferred_element_type=f32)


def aligned(index, size):
    return pl.ds(pl.multiple_of(index * size, size), size)


def flat(offset):
    dx, dz, dc = offset
    return dx * 4 + dz * 2 + dc


def back(offset):
    dx, dz, dc = offset
    return ((4 - dx) % 4, dz, dc)


def merged(factors, grams):
    rows = [None] * 4
    for p in (3, 2, 1, 0):
        unit = (lax.broadcasted_iota(jnp.int32, (128, 512), 0) + p * 128
                == lax.broadcasted_iota(jnp.int32, (128, 512), 1)).astype(f32)
        for q in range(p + 1, 4):
            unit = unit - exact(grams[PAIRS.index((p, q))], rows[q])
        rows[p] = exact(factors[p], unit)
    return jnp.concatenate(rows, axis=0)


def upper(t):
    keep = (lax.broadcasted_iota(jnp.int32, (128, 128), 0)
            <= lax.broadcasted_iota(jnp.int32, (128, 128), 1))
    return jnp.where(keep, t, 0.0)


def move_kernel(
    yl, yr, u, v, tl_in, tr_in,
    u_out, v_out, yl_out, yr_out, wl_out, wr_out,
    ubuf, vbuf, ylbuf, yrbuf, ylt_h, ylt_l, yrt_h, yrt_l,
    spr, core_in, x_in, shr, zl_in, wr,
    spl, y_in, shl, zh_in, wl,
    gl, gl_in, gl_sh, gl_z, gl_all, gr, gr_core, gr_sum, gr_in, gr_sh, gr_z, gr_all,
    tl_h, tl_l, tr_h, tr_l, tl, tr,
    lsem, osem, yls, ylr, yrs, yrr, us, ur, vs, vr,
    rs, rr, ls, lr, gls, glr, grs, grr,
):
    a = lax.axis_index("au")
    t = lax.axis_index("vert")
    y, zh = a // 2, a % 2
    x, zl, c = t // 4, (t // 2) % 2, t % 2

    def vpos(dx, dz, dc):
        return lax.rem(x + dx, 4) * 4 + lax.rem(zl + dz, 2) * 2 + lax.rem(c + dc, 2)

    def apos(dy, dz):
        return lax.rem(y + dy, 4) * 2 + lax.rem(zh + dz, 2)

    sent = []

    def send(src, dst, ssem, rsem, device):
        copy = pltpu.make_async_remote_copy(
            src_ref=src, dst_ref=dst, send_sem=ssem, recv_sem=rsem,
            device_id=device, device_id_type=MESH,
        )
        copy.start()
        sent.append(copy)

    def arrive(dst, sem):
        pltpu.make_async_remote_copy(
            src_ref=dst, dst_ref=dst, send_sem=sem, recv_sem=sem,
            device_id=(a, t), device_id_type=MESH,
        ).wait_recv()

    out_copies = []

    def put(src, dst, sem):
        copy = pltpu.make_async_copy(src, dst, sem)
        copy.start()
        out_copies.append(copy)

    locals_y = []
    for p in range(4):
        locals_y.append(pltpu.make_async_copy(
            yl.at[p], ylbuf.at[aligned(t, 128), pl.ds(p * 128, 128)], lsem.at[p]))
        locals_y.append(pltpu.make_async_copy(
            yr.at[p], yrbuf.at[aligned(a, 128), pl.ds(p * 128, 128)], lsem.at[4 + p]))
    local_u = pltpu.make_async_copy(u.at[:, aligned(t, 512)], ubuf.at[aligned(t, 128), :], lsem.at[8])
    local_v = pltpu.make_async_copy(v.at[:, aligned(a, 1024)], vbuf.at[aligned(a, 128), :], lsem.at[9])
    local_t = [pltpu.make_async_copy(tl_in, tl, lsem.at[10]), pltpu.make_async_copy(tr_in, tr, lsem.at[11])]
    for copy in locals_y + [local_u, local_v] + local_t:
        copy.start()

    barrier = pltpu.get_barrier_semaphore()
    for offset in VERT_OFFSETS:
        pl.semaphore_signal(barrier, inc=1, device_id=(a, vpos(*offset)), device_id_type=MESH)
    for o in range(1, 8):
        pl.semaphore_signal(barrier, inc=1, device_id=(apos(o // 2, o % 2), t), device_id_type=MESH)
    pl.semaphore_wait(barrier, 22)

    for copy in locals_y:
        copy.wait()

    def yl_slot(dx, dz, dc):
        return ylbuf.at[aligned(vpos(dx, dz, dc), 128), :]

    def yr_slot(dy, dz):
        return yrbuf.at[aligned(apos(dy, dz), 128), :]

    def send_v(part, o):
        dy, dz = o // 2, o % 2
        target = apos(dy, dz)
        begin, width = 2 * STARTS[part], 2 * PARTS[part]
        send(v.at[:, pl.ds(pl.multiple_of(target * 1024 + begin, 256), width)],
             vbuf.at[aligned(a, 128), pl.ds(begin, width)],
             vs.at[part, o], vr.at[part, ((4 - dy) % 4) * 2 + dz], (target, t))

    def send_u(part, offset):
        target = vpos(*offset)
        begin, width = STARTS[part], PARTS[part]
        send(u.at[:, pl.ds(pl.multiple_of(target * 512 + begin, 128), width)],
             ubuf.at[aligned(t, 128), pl.ds(begin, width)],
             us.at[part, flat(offset)], ur.at[part, flat(back(offset))], (a, target))

    def in_plane(part):
        for o in (2, 6, 4):
            send_v(part, o)
        for dc in (0, 1):
            for dx in (1, 3, 2):
                send_u(part, (dx, 0, dc))
        send_u(part, (0, 0, 1))

    def across(part):
        for o, dx in ((1, 0), (3, 1), (7, 3), (5, 2)):
            send_v(part, o)
            for dc in (0, 1):
                send_u(part, (dx, 1, dc))

    own = yl_slot(0, 0, 0)
    mine = yr_slot(0, 0)
    send(own, own, yls.at[0], ylr.at[2], (a, vpos(0, 1, 0)))
    send(mine, mine, yrs.at[0], yrr.at[1], (apos(0, 1), t))
    for d in (1, 3, 2):
        send(own, own, yls.at[d], ylr.at[((4 - d) % 4) * 4], (a, vpos(d, 0, 0)))
        send(mine, mine, yrs.at[d], yrr.at[((4 - d) % 4) * 2], (apos(d, 0), t))
    send(own, own, yls.at[7], ylr.at[1], (a, vpos(0, 0, 1)))

    slot = yl_slot(0, 1, 0)
    arrive(slot, ylr.at[2])
    for dx in (1, 3, 2):
        send(slot, slot, yls.at[3 + dx], ylr.at[((4 - dx) % 4) * 4 + 2], (a, vpos(dx, 0, 0)))
    send(slot, slot, yls.at[8], ylr.at[3], (a, vpos(0, 0, 1)))
    across(0)
    in_plane(0)
    for dz in (0, 1):
        for dx in (1, 3, 2):
            slot = yl_slot(dx, dz, 0)
            arrive(slot, ylr.at[dx * 4 + dz * 2])
            send(slot, slot, yls.at[8 + dz * 3 + dx], ylr.at[dx * 4 + dz * 2 + 1], (a, vpos(0, 0, 1)))

    def turn(source, high, low, count):
        def body(j, carry):
            high_part, low_part = split(source[aligned(j, 128), :].T)
            high[:, aligned(j, 128)] = high_part
            low[:, aligned(j, 128)] = low_part
            return carry
        lax.fori_loop(0, count, body, 0)

    def gram(high, low, out):
        def block(p, n, q, m):
            rows, cols = pl.ds(p * 128, n * 128), pl.ds(q * 128, m * 128)
            return three(high[rows, :], low[rows, :], high[cols, :], low[cols, :], dot_t)
        out[0:128, :] = block(0, 1, 1, 1)
        square = block(0, 2, 2, 2)
        out[128:256, :] = square[:128, :128]
        out[256:384, :] = square[:128, 128:]
        out[384:512, :] = square[128:, :128]
        out[512:640, :] = square[128:, 128:]
        out[640:768, :] = block(2, 1, 3, 1)

    def gram_left():
        for dy in (1, 3, 2):
            send(gl.at[aligned(lax.rem(y + dy, 4), 192), :], gl_in.at[(4 - dy) % 4 - 1],
                 gls.at[dy], glr.at[(4 - dy) % 4], (apos(dy, 0), t))

    def gram_right():
        arrive(gr_core, grr.at[0])
        gr_sum[...] = gr[...] + gr_core[...]
        for dx in (1, 3, 2):
            send(gr_sum.at[aligned(lax.rem(x + dx, 4), 192), :], gr_in.at[(4 - dx) % 4 - 1],
                 grs.at[dx], grr.at[(4 - dx) % 4], (a, vpos(dx, 0, 0)))

    def gram_pair_left():
        for dy in (1, 3, 2):
            arrive(gl_in.at[dy - 1], glr.at[dy])
        gl_sh[...] = gl[aligned(y, 192), :] + gl_in[0] + gl_in[1] + gl_in[2]
        send(gl_sh, gl_z, gls.at[4], glr.at[4], (apos(0, 1), t))

    def gram_pair_right():
        for dx in (1, 3, 2):
            arrive(gr_in.at[dx - 1], grr.at[dx])
        gr_sh[...] = gr_sum[aligned(x, 192), :] + gr_in[0] + gr_in[1] + gr_in[2]
        send(gr_sh, gr_z, grs.at[4], grr.at[4], (a, vpos(0, 1, 0)))

    def gram_spread_left():
        arrive(gl_z, glr.at[4])
        spot_l = gl_all.at[aligned(y, 192), :]
        spot_l[...] = gl_sh[...] + gl_z[...]
        for dy in (1, 3, 2):
            send(spot_l, spot_l, gls.at[4 + dy], glr.at[4 + (4 - dy) % 4], (apos(dy, 0), t))

    def gram_spread_right():
        arrive(gr_z, grr.at[4])
        spot_r = gr_all.at[aligned(x, 192), :]
        spot_r[...] = gr_sh[...] + gr_z[...]
        for dx in (1, 3, 2):
            send(spot_r, spot_r, grs.at[4 + dx], grr.at[4 + (4 - dx) % 4], (a, vpos(dx, 0, 0)))

    def merge_left():
        for dy in (1, 2, 3):
            arrive(gl_all.at[aligned(lax.rem(y + dy, 4), 192), :], glr.at[4 + dy])
        tl_h[...], tl_l[...] = split(merged(
            [upper(tl[p]) for p in range(4)], [gl_all[pl.ds(i * 128, 128), :] for i in range(6)]))

    def merge_right():
        for dx in (1, 2, 3):
            arrive(gr_all.at[aligned(lax.rem(x + dx, 4), 192), :], grr.at[4 + dx])
        tr_h[...], tr_l[...] = split(merged(
            [upper(tr[p]).T for p in range(4)], [gr_all[pl.ds(i * 128, 128), :] for i in range(6)]))

    for o in range(1, 16, 2):
        arrive(yl_slot(o // 4, (o // 2) % 2, 1), ylr.at[o])
    put(ylbuf, yl_out, osem.at[1])
    turn(ylbuf, ylt_h, ylt_l, 16)
    gram(ylt_h, ylt_l, gl)
    gram_left()

    slot = yr_slot(0, 1)
    arrive(slot, yrr.at[1])
    for dy in (1, 3, 2):
        send(slot, slot, yrs.at[3 + dy], yrr.at[((4 - dy) % 4) * 2 + 1], (apos(dy, 0), t))

    across(1)
    in_plane(1)

    for dz in (0, 1):
        for dy in (1, 3, 2):
            arrive(yr_slot(dy, dz), yrr.at[dy * 2 + dz])
    put(yrbuf, yr_out, osem.at[0])
    turn(yrbuf, yrt_h, yrt_l, 8)
    gram(yrt_h, yrt_l, gr)
    send(gr, gr_core, grs.at[0], grr.at[0], (a, vpos(0, 0, 1)))

    gram_right()
    for copy in local_t + [local_u, local_v]:
        copy.wait()
    def right_sums(part):
        begin, width = 2 * STARTS[part], 2 * PARTS[part]
        for o in range(1, 8):
            arrive(vbuf.at[aligned(apos(o // 2, o % 2), 128), pl.ds(begin, width)], vr.at[part, o])
        put(vbuf.at[:, pl.ds(begin, width)], v_out.at[:, pl.ds(begin, width)], osem.at[2 + part])

        def tile(n, carry):
            columns = pl.ds(pl.multiple_of(begin + n * 256, 256), 256)
            high, low = split(vbuf[:, columns])
            spr[columns, :] = three(yrt_h[...], yrt_l[...], high, low).T
            return carry
        lax.fori_loop(0, width // 256, tile, 0)
        half = PARTS[part]
        send(spr.at[pl.ds(pl.multiple_of(begin + (1 - c) * half, 128), half), :],
             core_in.at[pl.ds(STARTS[part], half), :], rs.at[part, 0], rr.at[part, 0], (a, vpos(0, 0, 1)))

    def right_share(part, core, row):
        half = PARTS[part]
        return pl.ds(pl.multiple_of(2 * STARTS[part] + core * half + row * (half // 4), 32), half // 4)

    def left_share(part, row):
        quarter = PARTS[part] // 4
        return pl.ds(pl.multiple_of(STARTS[part] + row * quarter, 32), quarter)

    def inner(part):
        return pl.ds(STARTS[part] // 4, PARTS[part] // 4)

    def right_core(part):
        half = PARTS[part]
        arrive(core_in.at[pl.ds(STARTS[part], half), :], rr.at[part, 0])
        mine = pl.ds(pl.multiple_of(2 * STARTS[part] + c * half, 128), half)
        spr[mine, :] += core_in[pl.ds(STARTS[part], half), :]
        for dx in (1, 3, 2):
            send(spr.at[right_share(part, c, lax.rem(x + dx, 4)), :], x_in.at[(4 - dx) % 4 - 1, inner(part), :],
                 rs.at[part, dx], rr.at[part, (4 - dx) % 4], (a, vpos(dx, 0, 0)))

    def right_pair(part):
        for dx in (1, 2, 3):
            arrive(x_in.at[dx - 1, inner(part), :], rr.at[part, dx])
        at = inner(part)
        shr[at, :] = spr[right_share(part, c, x), :] + x_in[0, at, :] + x_in[1, at, :] + x_in[2, at, :]
        send(shr.at[at, :], zl_in.at[at, :], rs.at[part, 4], rr.at[part, 4], (a, vpos(0, 1, 0)))

    def right_spread(part):
        at = inner(part)
        arrive(zl_in.at[at, :], rr.at[part, 4])
        high, low = split(shr[at, :] + zl_in[at, :])
        place = wr.at[right_share(part, c, x), :]
        place[...] = three(high, low, tr_h[...], tr_l[...], dot_t)
        for dx in (1, 3, 2):
            send(place, place, rs.at[part, 4 + dx], rr.at[part, 4 + (4 - dx) % 4], (a, vpos(dx, 0, 0)))
        send(place, place, rs.at[part, 8], rr.at[part, 8], (a, vpos(0, 0, 1)))

    def right_onward(part):
        for dx in (1, 3, 2):
            got = wr.at[right_share(part, c, lax.rem(x + dx, 4)), :]
            arrive(got, rr.at[part, 4 + dx])
            send(got, got, rs.at[part, 8 + dx], rr.at[part, 8 + dx], (a, vpos(0, 0, 1)))

    def right_done(part):
        for dx in (0, 1, 2, 3):
            arrive(wr.at[right_share(part, 1 - c, lax.rem(x + dx, 4)), :], rr.at[part, 8 + dx])

    def left_sums(part):
        begin, width = STARTS[part], PARTS[part]
        for offset in VERT_OFFSETS:
            arrive(ubuf.at[aligned(vpos(*offset), 128), pl.ds(begin, width)], ur.at[part, flat(offset)])
        put(ubuf.at[:, pl.ds(begin, width)], u_out.at[:, pl.ds(begin, width)], osem.at[4 + part])
        for tile in range(begin, begin + width, 256):
            columns = pl.ds(tile, min(256, begin + width - tile))
            high, low = split(ubuf[:, columns])
            spl[columns, :] = three(ylt_h[...], ylt_l[...], high, low).T
        for dy in (1, 3, 2):
            send(spl.at[left_share(part, lax.rem(y + dy, 4)), :], y_in.at[(4 - dy) % 4 - 1, inner(part), :],
                 ls.at[part, dy], lr.at[part, (4 - dy) % 4], (apos(dy, 0), t))

    def left_pair(part):
        at = inner(part)
        for dy in (1, 2, 3):
            arrive(y_in.at[dy - 1, at, :], lr.at[part, dy])
        shl[at, :] = spl[left_share(part, y), :] + y_in[0, at, :] + y_in[1, at, :] + y_in[2, at, :]
        send(shl.at[at, :], zh_in.at[at, :], ls.at[part, 4], lr.at[part, 4], (apos(0, 1), t))

    def left_spread(part):
        at = inner(part)
        arrive(zh_in.at[at, :], lr.at[part, 4])
        high, low = split(shl[at, :] + zh_in[at, :])
        place = wl.at[left_share(part, y), :]
        place[...] = three(high, low, tl_h[...], tl_l[...], dot_t)
        for dy in (1, 3, 2):
            send(place, place, ls.at[part, 4 + dy], lr.at[part, 4 + (4 - dy) % 4], (apos(dy, 0), t))

    def left_done(part):
        for dy in (1, 2, 3):
            arrive(wl.at[left_share(part, lax.rem(y + dy, 4)), :], lr.at[part, 4 + dy])

    right_sums(0)
    left_sums(0)
    right_core(0)
    gram_pair_right()
    gram_pair_left()
    right_sums(1)
    gram_spread_right()
    gram_spread_left()
    left_sums(1)
    right_core(1)
    merge_right()
    left_pair(0)
    right_pair(0)
    merge_left()
    left_pair(1)
    right_pair(1)
    left_spread(0)
    right_spread(0)
    left_spread(1)
    right_spread(1)
    right_onward(0)
    right_onward(1)
    for part in range(2):
        left_done(part)
        right_done(part)
    put(wr, wr_out, osem.at[6])
    put(wl, wl_out, osem.at[7])
    for copy in sent:
        copy.wait_send()
    for copy in out_copies:
        copy.wait()


def update_kernel(wl, yl, u, yr, v, wr, u_out, v_out, wl_h, wl_l, wr_h, wr_l):
    step = pl.program_id(0)

    @pl.when(step == 0)
    def _():
        wl_h[...], wl_l[...] = split(wl[...])

    @pl.when(step == 4)
    def _():
        wr_h[...], wr_l[...] = split(wr[...])

    @pl.when(step < 4)
    def _():
        high, low = split(yl[...])
        u_out[...] = u[...] - three(high, low, wl_h[...], wl_l[...], dot_t)

    @pl.when(step >= 4)
    def _():
        high, low = split(yr[...])
        v_out[...] = v[...] - three(high, low, wr_h[...], wr_l[...], dot_t)


def shards(u_band, v_band, y_left, t_left, y_right, t_right):
    any_space = pl.BlockSpec(memory_space=pl.ANY)
    shape = jax.ShapeDtypeStruct
    dma = pltpu.SemaphoreType.DMA
    buf = lambda *dims: pltpu.VMEM(dims, f32)
    half = lambda *dims: pltpu.VMEM(dims, bf16)
    u_all, v_all, yl_all, yr_all, w_left, w_right = pl.pallas_call(
        move_kernel,
        out_shape=[
            shape((2048, 512), f32), shape((1024, 1024), f32),
            shape((2048, 512), f32), shape((1024, 512), f32),
            shape((512, 512), f32), shape((1024, 512), f32),
        ],
        in_specs=[any_space] * 6,
        out_specs=[any_space] * 6,
        scratch_shapes=[
            buf(2048, 512), buf(1024, 1024), buf(2048, 512), buf(1024, 512),
            half(512, 2048), half(512, 2048), half(512, 1024), half(512, 1024),
            buf(1024, 512), buf(512, 512), buf(3, 128, 512), buf(128, 512), buf(128, 512), buf(1024, 512),
            buf(512, 512), buf(3, 128, 512), buf(128, 512), buf(128, 512), buf(512, 512),
            buf(768, 128), buf(3, 192, 128), buf(192, 128), buf(192, 128), buf(768, 128),
            buf(768, 128), buf(768, 128), buf(768, 128), buf(3, 192, 128), buf(192, 128), buf(192, 128), buf(768, 128),
            half(512, 512), half(512, 512), half(512, 512), half(512, 512),
            buf(4, 128, 128), buf(4, 128, 128),
            dma((12,)), dma((8,)), dma((16,)), dma((16,)), dma((8,)), dma((8,)),
            dma((len(PARTS), 16)), dma((len(PARTS), 16)), dma((len(PARTS), 8)), dma((len(PARTS), 8)),
            dma((len(PARTS), 12)), dma((len(PARTS), 12)), dma((len(PARTS), 8)), dma((len(PARTS), 8)),
            dma((8,)), dma((8,)), dma((8,)), dma((8,)),
        ],
        compiler_params=pltpu.CompilerParams(
            collective_id=0, has_side_effects=True, vmem_limit_bytes=60 * 2**20,
        ),
        cost_estimate=pl.CostEstimate(flops=2 * 10**10, bytes_accessed=4 * 10**8, transcendentals=0),
    )(y_left, y_right, u_band, v_band, t_left, t_right)

    first = lambda i: (jnp.minimum(i, 3), 0)
    second = lambda i: (jnp.maximum(i - 4, 0), 0)
    whole = lambda i: (0, 0)
    return pl.pallas_call(
        update_kernel,
        grid=(8,),
        out_shape=[shape((2048, 512), f32), shape((1024, 1024), f32)],
        in_specs=[
            pl.BlockSpec((512, 512), whole),
            pl.BlockSpec((512, 512), first), pl.BlockSpec((512, 512), first),
            pl.BlockSpec((256, 512), second), pl.BlockSpec((256, 1024), second),
            pl.BlockSpec((1024, 512), whole),
        ],
        out_specs=[pl.BlockSpec((512, 512), first), pl.BlockSpec((256, 1024), second)],
        scratch_shapes=[half(512, 512), half(512, 512), half(1024, 512), half(1024, 512)],
        compiler_params=pltpu.CompilerParams(vmem_limit_bytes=60 * 2**20),
    )(w_left, yl_all, u_all, yr_all, v_all, w_right)


def solution(mesh):
    return jax.shard_map(
        shards,
        mesh=mesh,
        in_specs=(
            P(("au", "vert"), None),
            P(("vert", "au"), None),
            P(None, ("au", "vert"), None),
            P(),
            P(None, ("vert", "au"), None),
            P(),
        ),
        out_specs=(P("au", "vert"), P("vert", "au")),
        check_vma=False,
    )
```

```python
import functools

import jax
import jax.numpy as jnp
from jax import lax
from jax.experimental import pallas as pl
from jax.experimental.pallas import tpu as pltpu
from jax.sharding import PartitionSpec as P

MESH = pl.DeviceIdType.MESH
f32 = jnp.float32
bf16 = jnp.bfloat16
PARTS = (256, 256)
STARTS = [sum(PARTS[:part]) for part in range(len(PARTS))]
PAIRS = [(0, 1), (0, 2), (0, 3), (1, 2), (1, 3), (2, 3)]
VERT_OFFSETS = [(dx, dz, dc) for dx in (2, 1, 3, 0) for dz in (1, 0) for dc in (0, 1)][:-2] + [(0, 0, 1)]


def split(value):
    high = value.astype(bf16)
    return high, (value - high.astype(f32)).astype(bf16)


def dot(a, b):
    return lax.dot_general(a, b, (((1,), (0,)), ((), ())), preferred_element_type=f32)


def dot_t(a, b):
    return lax.dot_general(a, b, (((1,), (1,)), ((), ())), preferred_element_type=f32)


def three(a_high, a_low, b_high, b_low, product=dot):
    return product(a_high, b_high) + product(a_high, b_low) + product(a_low, b_high)


def exact(a, b):
    return three(*split(a), *split(b))


def aligned(index, size):
    return pl.ds(pl.multiple_of(index * size, size), size)


def flat(offset):
    dx, dz, dc = offset
    return dx * 4 + dz * 2 + dc


def back(offset):
    dx, dz, dc = offset
    return ((4 - dx) % 4, dz, dc)


def merged(factors, grams):
    rows = [None] * 4
    for p in (3, 2, 1, 0):
        unit = (lax.broadcasted_iota(jnp.int32, (128, 512), 0) + p * 128
                == lax.broadcasted_iota(jnp.int32, (128, 512), 1)).astype(f32)
        if p < 3:
            beside = jnp.concatenate([grams[PAIRS.index((p, q))] for q in range(p + 1, 4)], axis=1)
            unit = unit - exact(beside, jnp.concatenate(rows[p + 1:], axis=0))
        rows[p] = exact(factors[p], unit)
    return jnp.concatenate(rows, axis=0)


def upper(t):
    keep = (lax.broadcasted_iota(jnp.int32, (128, 128), 0)
            <= lax.broadcasted_iota(jnp.int32, (128, 128), 1))
    return jnp.where(keep, t, 0.0)


def move_kernel(
    yl, yr, u, v, tl_in, tr_in,
    u_out, v_out, yl_out, yr_out, wl_out, wr_out,
    ubuf, vbuf, ylbuf, yrbuf, ylt_h, ylt_l, yrt_h, yrt_l,
    spr, core_in, x_in, shr, zl_in, wr,
    spl, y_in, shl, zh_in, wl,
    gl, gl_in, gl_sh, gl_z, gl_all, gr, gr_core, gr_sum, gr_in, gr_sh, gr_z, gr_all,
    tl_h, tl_l, tr_h, tr_l, tl, tr,
    lsem, osem, yls, ylr, yrs, yrr, us, ur, vs, vr,
    rs, rr, ls, lr, gls, glr, grs, grr,
):
    a = lax.axis_index("au")
    t = lax.axis_index("vert")
    y, zh = a // 2, a % 2
    x, zl, c = t // 4, (t // 2) % 2, t % 2

    def vpos(dx, dz, dc):
        return lax.rem(x + dx, 4) * 4 + lax.rem(zl + dz, 2) * 2 + lax.rem(c + dc, 2)

    def apos(dy, dz):
        return lax.rem(y + dy, 4) * 2 + lax.rem(zh + dz, 2)

    sent = []

    def send(src, dst, ssem, rsem, device):
        copy = pltpu.make_async_remote_copy(
            src_ref=src, dst_ref=dst, send_sem=ssem, recv_sem=rsem,
            device_id=device, device_id_type=MESH,
        )
        copy.start()
        sent.append(copy)

    def arrive(dst, sem):
        pltpu.make_async_remote_copy(
            src_ref=dst, dst_ref=dst, send_sem=sem, recv_sem=sem,
            device_id=(a, t), device_id_type=MESH,
        ).wait_recv()

    out_copies = []

    def put(src, dst, sem):
        copy = pltpu.make_async_copy(src, dst, sem)
        copy.start()
        out_copies.append(copy)

    locals_y = []
    for p in range(4):
        locals_y.append(pltpu.make_async_copy(
            yl.at[p], ylbuf.at[aligned(t, 128), pl.ds(p * 128, 128)], lsem.at[p]))
        locals_y.append(pltpu.make_async_copy(
            yr.at[p], yrbuf.at[aligned(a, 128), pl.ds(p * 128, 128)], lsem.at[4 + p]))
    local_u = pltpu.make_async_copy(u.at[:, aligned(t, 512)], ubuf.at[aligned(t, 128), :], lsem.at[8])
    local_v = pltpu.make_async_copy(v.at[:, aligned(a, 1024)], vbuf.at[aligned(a, 128), :], lsem.at[9])
    local_t = [pltpu.make_async_copy(tl_in, tl, lsem.at[10]), pltpu.make_async_copy(tr_in, tr, lsem.at[11])]
    for copy in locals_y + [local_u, local_v] + local_t:
        copy.start()

    barrier = pltpu.get_barrier_semaphore()
    for offset in VERT_OFFSETS:
        pl.semaphore_signal(barrier, inc=1, device_id=(a, vpos(*offset)), device_id_type=MESH)
    for o in range(1, 8):
        pl.semaphore_signal(barrier, inc=1, device_id=(apos(o // 2, o % 2), t), device_id_type=MESH)
    pl.semaphore_wait(barrier, 22)

    for copy in locals_y:
        copy.wait()

    def yl_slot(dx, dz, dc):
        return ylbuf.at[aligned(vpos(dx, dz, dc), 128), :]

    def yr_slot(dy, dz):
        return yrbuf.at[aligned(apos(dy, dz), 128), :]

    def send_v(part, o):
        dy, dz = o // 2, o % 2
        target = apos(dy, dz)
        begin, width = 2 * STARTS[part], 2 * PARTS[part]
        send(v.at[:, pl.ds(pl.multiple_of(target * 1024 + begin, 256), width)],
             vbuf.at[aligned(a, 128), pl.ds(begin, width)],
             vs.at[part, o], vr.at[part, ((4 - dy) % 4) * 2 + dz], (target, t))

    def send_u(part, offset):
        target = vpos(*offset)
        begin, width = STARTS[part], PARTS[part]
        send(u.at[:, pl.ds(pl.multiple_of(target * 512 + begin, 128), width)],
             ubuf.at[aligned(t, 128), pl.ds(begin, width)],
             us.at[part, flat(offset)], ur.at[part, flat(back(offset))], (a, target))

    def in_plane(part):
        for o in (2, 6, 4):
            send_v(part, o)
        for dc in (0, 1):
            for dx in (1, 3, 2):
                send_u(part, (dx, 0, dc))
        send_u(part, (0, 0, 1))

    def across(part):
        for o, dx in ((1, 0), (3, 1), (7, 3), (5, 2)):
            send_v(part, o)
            for dc in (0, 1):
                send_u(part, (dx, 1, dc))

    own = yl_slot(0, 0, 0)
    mine = yr_slot(0, 0)
    send(own, own, yls.at[0], ylr.at[2], (a, vpos(0, 1, 0)))
    send(mine, mine, yrs.at[0], yrr.at[1], (apos(0, 1), t))
    for d in (1, 3, 2):
        send(own, own, yls.at[d], ylr.at[((4 - d) % 4) * 4], (a, vpos(d, 0, 0)))
        send(mine, mine, yrs.at[d], yrr.at[((4 - d) % 4) * 2], (apos(d, 0), t))
    send(own, own, yls.at[7], ylr.at[1], (a, vpos(0, 0, 1)))

    slot = yl_slot(0, 1, 0)
    arrive(slot, ylr.at[2])
    for dx in (1, 3, 2):
        send(slot, slot, yls.at[3 + dx], ylr.at[((4 - dx) % 4) * 4 + 2], (a, vpos(dx, 0, 0)))
    send(slot, slot, yls.at[8], ylr.at[3], (a, vpos(0, 0, 1)))
    across(0)
    in_plane(0)
    for dz in (0, 1):
        for dx in (1, 3, 2):
            slot = yl_slot(dx, dz, 0)
            arrive(slot, ylr.at[dx * 4 + dz * 2])
            send(slot, slot, yls.at[8 + dz * 3 + dx], ylr.at[dx * 4 + dz * 2 + 1], (a, vpos(0, 0, 1)))

    def turn(source, high, low, count):
        def body(j, carry):
            high_part, low_part = split(source[aligned(j, 128), :].T)
            high[:, aligned(j, 128)] = high_part
            low[:, aligned(j, 128)] = low_part
            return carry
        lax.fori_loop(0, count, body, 0)

    def gram(high, low, out):
        def block(p, n, q, m):
            rows, cols = pl.ds(p * 128, n * 128), pl.ds(q * 128, m * 128)
            return three(high[rows, :], low[rows, :], high[cols, :], low[cols, :], dot_t)
        out[0:128, :] = block(0, 1, 1, 1)
        square = block(0, 2, 2, 2)
        out[128:256, :] = square[:128, :128]
        out[256:384, :] = square[:128, 128:]
        out[384:512, :] = square[128:, :128]
        out[512:640, :] = square[128:, 128:]
        out[640:768, :] = block(2, 1, 3, 1)

    def gram_left():
        for dy in (1, 3, 2):
            send(gl.at[aligned(lax.rem(y + dy, 4), 192), :], gl_in.at[(4 - dy) % 4 - 1],
                 gls.at[dy], glr.at[(4 - dy) % 4], (apos(dy, 0), t))

    def gram_right():
        arrive(gr_core, grr.at[0])
        gr_sum[...] = gr[...] + gr_core[...]
        for dx in (1, 3, 2):
            send(gr_sum.at[aligned(lax.rem(x + dx, 4), 192), :], gr_in.at[(4 - dx) % 4 - 1],
                 grs.at[dx], grr.at[(4 - dx) % 4], (a, vpos(dx, 0, 0)))

    def gram_pair_left():
        for dy in (1, 3, 2):
            arrive(gl_in.at[dy - 1], glr.at[dy])
        gl_sh[...] = gl[aligned(y, 192), :] + gl_in[0] + gl_in[1] + gl_in[2]
        send(gl_sh, gl_z, gls.at[4], glr.at[4], (apos(0, 1), t))

    def gram_pair_right():
        for dx in (1, 3, 2):
            arrive(gr_in.at[dx - 1], grr.at[dx])
        gr_sh[...] = gr_sum[aligned(x, 192), :] + gr_in[0] + gr_in[1] + gr_in[2]
        send(gr_sh, gr_z, grs.at[4], grr.at[4], (a, vpos(0, 1, 0)))

    def gram_spread_left():
        arrive(gl_z, glr.at[4])
        spot_l = gl_all.at[aligned(y, 192), :]
        spot_l[...] = gl_sh[...] + gl_z[...]
        for dy in (1, 3, 2):
            send(spot_l, spot_l, gls.at[4 + dy], glr.at[4 + (4 - dy) % 4], (apos(dy, 0), t))

    def gram_spread_right():
        arrive(gr_z, grr.at[4])
        spot_r = gr_all.at[aligned(x, 192), :]
        spot_r[...] = gr_sh[...] + gr_z[...]
        for dx in (1, 3, 2):
            send(spot_r, spot_r, grs.at[4 + dx], grr.at[4 + (4 - dx) % 4], (a, vpos(dx, 0, 0)))

    def merge_left():
        for dy in (1, 2, 3):
            arrive(gl_all.at[aligned(lax.rem(y + dy, 4), 192), :], glr.at[4 + dy])
        tl_h[...], tl_l[...] = split(merged(
            [upper(tl[p]) for p in range(4)], [gl_all[pl.ds(i * 128, 128), :] for i in range(6)]))

    def merge_right():
        for dx in (1, 2, 3):
            arrive(gr_all.at[aligned(lax.rem(x + dx, 4), 192), :], grr.at[4 + dx])
        tr_h[...], tr_l[...] = split(merged(
            [upper(tr[p]).T for p in range(4)], [gr_all[pl.ds(i * 128, 128), :] for i in range(6)]))

    for o in range(1, 16, 2):
        arrive(yl_slot(o // 4, (o // 2) % 2, 1), ylr.at[o])
    put(ylbuf, yl_out, osem.at[1])
    turn(ylbuf, ylt_h, ylt_l, 16)
    gram(ylt_h, ylt_l, gl)
    gram_left()

    slot = yr_slot(0, 1)
    arrive(slot, yrr.at[1])
    for dy in (1, 3, 2):
        send(slot, slot, yrs.at[3 + dy], yrr.at[((4 - dy) % 4) * 2 + 1], (apos(dy, 0), t))

    across(1)
    in_plane(1)

    for dz in (0, 1):
        for dy in (1, 3, 2):
            arrive(yr_slot(dy, dz), yrr.at[dy * 2 + dz])
    put(yrbuf, yr_out, osem.at[0])
    turn(yrbuf, yrt_h, yrt_l, 8)
    gram(yrt_h, yrt_l, gr)
    send(gr, gr_core, grs.at[0], grr.at[0], (a, vpos(0, 0, 1)))

    gram_right()
    for copy in local_t + [local_u, local_v]:
        copy.wait()
    def right_sums(part):
        begin, width = 2 * STARTS[part], 2 * PARTS[part]
        for o in range(1, 8):
            arrive(vbuf.at[aligned(apos(o // 2, o % 2), 128), pl.ds(begin, width)], vr.at[part, o])
        put(vbuf.at[:, pl.ds(begin, width)], v_out.at[:, pl.ds(begin, width)], osem.at[2 + part])

        def tile(n, carry):
            columns = pl.ds(pl.multiple_of(begin + n * 256, 256), 256)
            high, low = split(vbuf[:, columns])
            spr[columns, :] = three(yrt_h[...], yrt_l[...], high, low).T
            return carry
        lax.fori_loop(0, width // 256, tile, 0)
        half = PARTS[part]
        send(spr.at[pl.ds(pl.multiple_of(begin + (1 - c) * half, 128), half), :],
             core_in.at[pl.ds(STARTS[part], half), :], rs.at[part, 0], rr.at[part, 0], (a, vpos(0, 0, 1)))

    def right_share(part, core, row):
        half = PARTS[part]
        return pl.ds(pl.multiple_of(2 * STARTS[part] + core * half + row * (half // 4), 32), half // 4)

    def left_share(part, row):
        quarter = PARTS[part] // 4
        return pl.ds(pl.multiple_of(STARTS[part] + row * quarter, 32), quarter)

    def inner(part):
        return pl.ds(STARTS[part] // 4, PARTS[part] // 4)

    def right_core(part):
        half = PARTS[part]
        arrive(core_in.at[pl.ds(STARTS[part], half), :], rr.at[part, 0])
        mine = pl.ds(pl.multiple_of(2 * STARTS[part] + c * half, 128), half)
        spr[mine, :] += core_in[pl.ds(STARTS[part], half), :]
        for dx in (1, 3, 2):
            send(spr.at[right_share(part, c, lax.rem(x + dx, 4)), :], x_in.at[(4 - dx) % 4 - 1, inner(part), :],
                 rs.at[part, dx], rr.at[part, (4 - dx) % 4], (a, vpos(dx, 0, 0)))

    def right_pair(part):
        for dx in (1, 2, 3):
            arrive(x_in.at[dx - 1, inner(part), :], rr.at[part, dx])
        at = inner(part)
        shr[at, :] = spr[right_share(part, c, x), :] + x_in[0, at, :] + x_in[1, at, :] + x_in[2, at, :]
        send(shr.at[at, :], zl_in.at[at, :], rs.at[part, 4], rr.at[part, 4], (a, vpos(0, 1, 0)))

    def right_spread(part):
        at = inner(part)
        arrive(zl_in.at[at, :], rr.at[part, 4])
        high, low = split(shr[at, :] + zl_in[at, :])
        place = wr.at[right_share(part, c, x), :]
        place[...] = three(high, low, tr_h[...], tr_l[...], dot_t)
        for dx in (1, 3, 2):
            send(place, place, rs.at[part, 4 + dx], rr.at[part, 4 + (4 - dx) % 4], (a, vpos(dx, 0, 0)))
        send(place, place, rs.at[part, 8], rr.at[part, 8], (a, vpos(0, 0, 1)))

    def right_onward(part):
        for dx in (1, 3, 2):
            got = wr.at[right_share(part, c, lax.rem(x + dx, 4)), :]
            arrive(got, rr.at[part, 4 + dx])
            send(got, got, rs.at[part, 8 + dx], rr.at[part, 8 + dx], (a, vpos(0, 0, 1)))

    def right_done(part):
        for dx in (0, 1, 2, 3):
            arrive(wr.at[right_share(part, 1 - c, lax.rem(x + dx, 4)), :], rr.at[part, 8 + dx])

    def left_sums(part):
        begin, width = STARTS[part], PARTS[part]
        for offset in VERT_OFFSETS:
            arrive(ubuf.at[aligned(vpos(*offset), 128), pl.ds(begin, width)], ur.at[part, flat(offset)])
        put(ubuf.at[:, pl.ds(begin, width)], u_out.at[:, pl.ds(begin, width)], osem.at[4 + part])
        for tile in range(begin, begin + width, 256):
            columns = pl.ds(tile, min(256, begin + width - tile))
            high, low = split(ubuf[:, columns])
            spl[columns, :] = three(ylt_h[...], ylt_l[...], high, low).T
        for dy in (1, 3, 2):
            send(spl.at[left_share(part, lax.rem(y + dy, 4)), :], y_in.at[(4 - dy) % 4 - 1, inner(part), :],
                 ls.at[part, dy], lr.at[part, (4 - dy) % 4], (apos(dy, 0), t))

    def left_pair(part):
        at = inner(part)
        for dy in (1, 2, 3):
            arrive(y_in.at[dy - 1, at, :], lr.at[part, dy])
        shl[at, :] = spl[left_share(part, y), :] + y_in[0, at, :] + y_in[1, at, :] + y_in[2, at, :]
        send(shl.at[at, :], zh_in.at[at, :], ls.at[part, 4], lr.at[part, 4], (apos(0, 1), t))

    def left_spread(part):
        at = inner(part)
        arrive(zh_in.at[at, :], lr.at[part, 4])
        high, low = split(shl[at, :] + zh_in[at, :])
        place = wl.at[left_share(part, y), :]
        place[...] = three(high, low, tl_h[...], tl_l[...], dot_t)
        for dy in (1, 3, 2):
            send(place, place, ls.at[part, 4 + dy], lr.at[part, 4 + (4 - dy) % 4], (apos(dy, 0), t))

    def left_done(part):
        for dy in (1, 2, 3):
            arrive(wl.at[left_share(part, lax.rem(y + dy, 4)), :], lr.at[part, 4 + dy])

    right_sums(0)
    left_sums(0)
    right_core(0)
    gram_pair_right()
    gram_pair_left()
    right_sums(1)
    gram_spread_right()
    gram_spread_left()
    left_sums(1)
    right_core(1)
    merge_right()
    right_pair(0)
    left_pair(0)
    merge_left()
    right_pair(1)
    left_pair(1)
    right_spread(0)
    left_spread(0)
    right_spread(1)
    left_spread(1)
    right_onward(0)
    right_onward(1)
    for part in range(2):
        left_done(part)
        right_done(part)
    put(wr, wr_out, osem.at[6])
    put(wl, wl_out, osem.at[7])
    for copy in sent:
        copy.wait_send()
    for copy in out_copies:
        copy.wait()


def update_kernel(wl, yl, u, yr, v, wr, u_out, v_out, wl_h, wl_l, wr_h, wr_l):
    step = pl.program_id(0)

    @pl.when(step == 0)
    def _():
        wl_h[...], wl_l[...] = split(wl[...])

    @pl.when(step == 4)
    def _():
        wr_h[...], wr_l[...] = split(wr[...])

    @pl.when(step < 4)
    def _():
        high, low = split(yl[...])
        u_out[...] = u[...] - three(high, low, wl_h[...], wl_l[...], dot_t)

    @pl.when(step >= 4)
    def _():
        high, low = split(yr[...])
        v_out[...] = v[...] - three(high, low, wr_h[...], wr_l[...], dot_t)


def shards(u_band, v_band, y_left, t_left, y_right, t_right):
    any_space = pl.BlockSpec(memory_space=pl.ANY)
    shape = jax.ShapeDtypeStruct
    dma = pltpu.SemaphoreType.DMA
    buf = lambda *dims: pltpu.VMEM(dims, f32)
    half = lambda *dims: pltpu.VMEM(dims, bf16)
    u_all, v_all, yl_all, yr_all, w_left, w_right = pl.pallas_call(
        move_kernel,
        out_shape=[
            shape((2048, 512), f32), shape((1024, 1024), f32),
            shape((2048, 512), f32), shape((1024, 512), f32),
            shape((512, 512), f32), shape((1024, 512), f32),
        ],
        in_specs=[any_space] * 6,
        out_specs=[any_space] * 6,
        scratch_shapes=[
            buf(2048, 512), buf(1024, 1024), buf(2048, 512), buf(1024, 512),
            half(512, 2048), half(512, 2048), half(512, 1024), half(512, 1024),
            buf(1024, 512), buf(512, 512), buf(3, 128, 512), buf(128, 512), buf(128, 512), buf(1024, 512),
            buf(512, 512), buf(3, 128, 512), buf(128, 512), buf(128, 512), buf(512, 512),
            buf(768, 128), buf(3, 192, 128), buf(192, 128), buf(192, 128), buf(768, 128),
            buf(768, 128), buf(768, 128), buf(768, 128), buf(3, 192, 128), buf(192, 128), buf(192, 128), buf(768, 128),
            half(512, 512), half(512, 512), half(512, 512), half(512, 512),
            buf(4, 128, 128), buf(4, 128, 128),
            dma((12,)), dma((8,)), dma((16,)), dma((16,)), dma((8,)), dma((8,)),
            dma((len(PARTS), 16)), dma((len(PARTS), 16)), dma((len(PARTS), 8)), dma((len(PARTS), 8)),
            dma((len(PARTS), 12)), dma((len(PARTS), 12)), dma((len(PARTS), 8)), dma((len(PARTS), 8)),
            dma((8,)), dma((8,)), dma((8,)), dma((8,)),
        ],
        compiler_params=pltpu.CompilerParams(
            collective_id=0, has_side_effects=True, vmem_limit_bytes=60 * 2**20,
        ),
        cost_estimate=pl.CostEstimate(flops=2 * 10**10, bytes_accessed=4 * 10**8, transcendentals=0),
    )(y_left, y_right, u_band, v_band, t_left, t_right)

    first = lambda i: (jnp.minimum(i, 3), 0)
    second = lambda i: (jnp.maximum(i - 4, 0), 0)
    whole = lambda i: (0, 0)
    return pl.pallas_call(
        update_kernel,
        grid=(8,),
        out_shape=[shape((2048, 512), f32), shape((1024, 1024), f32)],
        in_specs=[
            pl.BlockSpec((512, 512), whole),
            pl.BlockSpec((512, 512), first), pl.BlockSpec((512, 512), first),
            pl.BlockSpec((256, 512), second), pl.BlockSpec((256, 1024), second),
            pl.BlockSpec((1024, 512), whole),
        ],
        out_specs=[pl.BlockSpec((512, 512), first), pl.BlockSpec((256, 1024), second)],
        scratch_shapes=[half(512, 512), half(512, 512), half(1024, 512), half(1024, 512)],
        compiler_params=pltpu.CompilerParams(vmem_limit_bytes=60 * 2**20),
    )(w_left, yl_all, u_all, yr_all, v_all, w_right)


def solution(mesh):
    return jax.shard_map(
        shards,
        mesh=mesh,
        in_specs=(
            P(("au", "vert"), None),
            P(("vert", "au"), None),
            P(None, ("au", "vert"), None),
            P(),
            P(None, ("vert", "au"), None),
            P(),
        ),
        out_specs=(P("au", "vert"), P("vert", "au")),
        check_vma=False,
    )
```

```python
import functools

import jax
import jax.numpy as jnp
from jax import lax
from jax.experimental import pallas as pl
from jax.experimental.pallas import tpu as pltpu
from jax.sharding import PartitionSpec as P

MESH = pl.DeviceIdType.MESH
f32 = jnp.float32
bf16 = jnp.bfloat16
PARTS = (256, 256)
STARTS = [sum(PARTS[:part]) for part in range(len(PARTS))]
PAIRS = [(0, 1), (0, 2), (0, 3), (1, 2), (1, 3), (2, 3)]
VERT_OFFSETS = [(dx, dz, dc) for dx in (2, 1, 3, 0) for dz in (1, 0) for dc in (0, 1)][:-2] + [(0, 0, 1)]


def split(value):
    high = value.astype(bf16)
    return high, (value - high.astype(f32)).astype(bf16)


def dot(a, b):
    return lax.dot_general(a, b, (((1,), (0,)), ((), ())), preferred_element_type=f32)


def dot_t(a, b):
    return lax.dot_general(a, b, (((1,), (1,)), ((), ())), preferred_element_type=f32)


def three(a_high, a_low, b_high, b_low, product=dot):
    return product(a_high, b_high) + product(a_high, b_low) + product(a_low, b_high)


def exact(a, b):
    return three(*split(a), *split(b))


def aligned(index, size):
    return pl.ds(pl.multiple_of(index * size, size), size)


def flat(offset):
    dx, dz, dc = offset
    return dx * 4 + dz * 2 + dc


def back(offset):
    dx, dz, dc = offset
    return ((4 - dx) % 4, dz, dc)


def merged(factors, grams):
    rows = [None] * 4
    for p in (3, 2, 1, 0):
        unit = (lax.broadcasted_iota(jnp.int32, (128, 512), 0) + p * 128
                == lax.broadcasted_iota(jnp.int32, (128, 512), 1)).astype(f32)
        if p < 3:
            beside = jnp.concatenate([grams[PAIRS.index((p, q))] for q in range(p + 1, 4)], axis=1)
            unit = unit - exact(beside, jnp.concatenate(rows[p + 1:], axis=0))
        rows[p] = exact(factors[p], unit)
    return jnp.concatenate(rows, axis=0)


def upper(t):
    keep = (lax.broadcasted_iota(jnp.int32, (128, 128), 0)
            <= lax.broadcasted_iota(jnp.int32, (128, 128), 1))
    return jnp.where(keep, t, 0.0)


def move_kernel(
    yl, yr, u, v, tl_in, tr_in,
    u_out, v_out, yl_out, yr_out, wl_out, wr_out,
    ubuf, vbuf, ylbuf, yrbuf, ylt_h, ylt_l, yrt_h, yrt_l,
    spr, core_in, x_in, shr, zl_in, wr,
    spl, y_in, shl, zh_in, wl,
    gl, gl_in, gl_sh, gl_z, gl_all, gr, gr_core, gr_sum, gr_in, gr_sh, gr_z, gr_all,
    tl_h, tl_l, tr_h, tr_l, tl, tr,
    lsem, osem, yls, ylr, yrs, yrr, us, ur, vs, vr,
    rs, rr, ls, lr, gls, glr, grs, grr,
):
    a = lax.axis_index("au")
    t = lax.axis_index("vert")
    y, zh = a // 2, a % 2
    x, zl, c = t // 4, (t // 2) % 2, t % 2

    def vpos(dx, dz, dc):
        return lax.rem(x + dx, 4) * 4 + lax.rem(zl + dz, 2) * 2 + lax.rem(c + dc, 2)

    def apos(dy, dz):
        return lax.rem(y + dy, 4) * 2 + lax.rem(zh + dz, 2)

    sent = []

    def send(src, dst, ssem, rsem, device):
        copy = pltpu.make_async_remote_copy(
            src_ref=src, dst_ref=dst, send_sem=ssem, recv_sem=rsem,
            device_id=device, device_id_type=MESH,
        )
        copy.start()
        sent.append(copy)

    def arrive(dst, sem):
        pltpu.make_async_remote_copy(
            src_ref=dst, dst_ref=dst, send_sem=sem, recv_sem=sem,
            device_id=(a, t), device_id_type=MESH,
        ).wait_recv()

    out_copies = []

    def put(src, dst, sem):
        copy = pltpu.make_async_copy(src, dst, sem)
        copy.start()
        out_copies.append(copy)

    locals_y = []
    for p in range(4):
        locals_y.append(pltpu.make_async_copy(
            yl.at[p], ylbuf.at[aligned(t, 128), pl.ds(p * 128, 128)], lsem.at[p]))
        locals_y.append(pltpu.make_async_copy(
            yr.at[p], yrbuf.at[aligned(a, 128), pl.ds(p * 128, 128)], lsem.at[4 + p]))
    local_u = pltpu.make_async_copy(u.at[:, aligned(t, 512)], ubuf.at[aligned(t, 128), :], lsem.at[8])
    local_v = pltpu.make_async_copy(v.at[:, aligned(a, 1024)], vbuf.at[aligned(a, 128), :], lsem.at[9])
    local_t = [pltpu.make_async_copy(tl_in, tl, lsem.at[10]), pltpu.make_async_copy(tr_in, tr, lsem.at[11])]
    for copy in locals_y + [local_u, local_v] + local_t:
        copy.start()

    barrier = pltpu.get_barrier_semaphore()
    for offset in VERT_OFFSETS:
        pl.semaphore_signal(barrier, inc=1, device_id=(a, vpos(*offset)), device_id_type=MESH)
    for o in range(1, 8):
        pl.semaphore_signal(barrier, inc=1, device_id=(apos(o // 2, o % 2), t), device_id_type=MESH)
    pl.semaphore_wait(barrier, 22)

    for copy in locals_y:
        copy.wait()

    def yl_slot(dx, dz, dc):
        return ylbuf.at[aligned(vpos(dx, dz, dc), 128), :]

    def yr_slot(dy, dz):
        return yrbuf.at[aligned(apos(dy, dz), 128), :]

    def send_v(part, o):
        dy, dz = o // 2, o % 2
        target = apos(dy, dz)
        begin, width = 2 * STARTS[part], 2 * PARTS[part]
        send(v.at[:, pl.ds(pl.multiple_of(target * 1024 + begin, 256), width)],
             vbuf.at[aligned(a, 128), pl.ds(begin, width)],
             vs.at[part, o], vr.at[part, ((4 - dy) % 4) * 2 + dz], (target, t))

    def send_u(part, offset):
        target = vpos(*offset)
        begin, width = STARTS[part], PARTS[part]
        send(u.at[:, pl.ds(pl.multiple_of(target * 512 + begin, 128), width)],
             ubuf.at[aligned(t, 128), pl.ds(begin, width)],
             us.at[part, flat(offset)], ur.at[part, flat(back(offset))], (a, target))

    def in_plane(part):
        for o in (2, 6, 4):
            send_v(part, o)
        for dc in (0, 1):
            for dx in (1, 3, 2):
                send_u(part, (dx, 0, dc))
        send_u(part, (0, 0, 1))

    def across(part):
        for o, dx in ((1, 0), (3, 1), (7, 3), (5, 2)):
            send_v(part, o)
            for dc in (0, 1):
                send_u(part, (dx, 1, dc))

    own = yl_slot(0, 0, 0)
    mine = yr_slot(0, 0)
    send(own, own, yls.at[0], ylr.at[2], (a, vpos(0, 1, 0)))
    send(mine, mine, yrs.at[0], yrr.at[1], (apos(0, 1), t))
    for d in (1, 3, 2):
        send(own, own, yls.at[d], ylr.at[((4 - d) % 4) * 4], (a, vpos(d, 0, 0)))
        send(mine, mine, yrs.at[d], yrr.at[((4 - d) % 4) * 2], (apos(d, 0), t))
    send(own, own, yls.at[7], ylr.at[1], (a, vpos(0, 0, 1)))

    slot = yl_slot(0, 1, 0)
    arrive(slot, ylr.at[2])
    for dx in (1, 3, 2):
        send(slot, slot, yls.at[3 + dx], ylr.at[((4 - dx) % 4) * 4 + 2], (a, vpos(dx, 0, 0)))
    send(slot, slot, yls.at[8], ylr.at[3], (a, vpos(0, 0, 1)))
    across(0)
    in_plane(0)
    for dz in (0, 1):
        for dx in (1, 3, 2):
            slot = yl_slot(dx, dz, 0)
            arrive(slot, ylr.at[dx * 4 + dz * 2])
            send(slot, slot, yls.at[8 + dz * 3 + dx], ylr.at[dx * 4 + dz * 2 + 1], (a, vpos(0, 0, 1)))

    def turn(source, high, low, count):
        def body(j, carry):
            high_part, low_part = split(source[aligned(j, 128), :].T)
            high[:, aligned(j, 128)] = high_part
            low[:, aligned(j, 128)] = low_part
            return carry
        lax.fori_loop(0, count, body, 0)

    def gram(high, low, out):
        def block(p, n, q, m):
            rows, cols = pl.ds(p * 128, n * 128), pl.ds(q * 128, m * 128)
            return three(high[rows, :], low[rows, :], high[cols, :], low[cols, :], dot_t)
        out[0:128, :] = block(0, 1, 1, 1)
        square = block(0, 2, 2, 2)
        out[128:256, :] = square[:128, :128]
        out[256:384, :] = square[:128, 128:]
        out[384:512, :] = square[128:, :128]
        out[512:640, :] = square[128:, 128:]
        out[640:768, :] = block(2, 1, 3, 1)

    def gram_left():
        for dy in (1, 3, 2):
            send(gl.at[aligned(lax.rem(y + dy, 4), 192), :], gl_in.at[(4 - dy) % 4 - 1],
                 gls.at[dy], glr.at[(4 - dy) % 4], (apos(dy, 0), t))

    def gram_right():
        arrive(gr_core, grr.at[0])
        gr_sum[...] = gr[...] + gr_core[...]
        for dx in (1, 3, 2):
            send(gr_sum.at[aligned(lax.rem(x + dx, 4), 192), :], gr_in.at[(4 - dx) % 4 - 1],
                 grs.at[dx], grr.at[(4 - dx) % 4], (a, vpos(dx, 0, 0)))

    def gram_pair_left():
        for dy in (1, 3, 2):
            arrive(gl_in.at[dy - 1], glr.at[dy])
        gl_sh[...] = gl[aligned(y, 192), :] + gl_in[0] + gl_in[1] + gl_in[2]
        send(gl_sh, gl_z, gls.at[4], glr.at[4], (apos(0, 1), t))

    def gram_pair_right():
        for dx in (1, 3, 2):
            arrive(gr_in.at[dx - 1], grr.at[dx])
        gr_sh[...] = gr_sum[aligned(x, 192), :] + gr_in[0] + gr_in[1] + gr_in[2]
        send(gr_sh, gr_z, grs.at[4], grr.at[4], (a, vpos(0, 1, 0)))

    def gram_spread_left():
        arrive(gl_z, glr.at[4])
        spot_l = gl_all.at[aligned(y, 192), :]
        spot_l[...] = gl_sh[...] + gl_z[...]
        for dy in (1, 3, 2):
            send(spot_l, spot_l, gls.at[4 + dy], glr.at[4 + (4 - dy) % 4], (apos(dy, 0), t))

    def gram_spread_right():
        arrive(gr_z, grr.at[4])
        spot_r = gr_all.at[aligned(x, 192), :]
        spot_r[...] = gr_sh[...] + gr_z[...]
        for dx in (1, 3, 2):
            send(spot_r, spot_r, grs.at[4 + dx], grr.at[4 + (4 - dx) % 4], (a, vpos(dx, 0, 0)))

    def merge_left():
        for dy in (1, 2, 3):
            arrive(gl_all.at[aligned(lax.rem(y + dy, 4), 192), :], glr.at[4 + dy])
        tl_h[...], tl_l[...] = split(merged(
            [upper(tl[p]) for p in range(4)], [gl_all[pl.ds(i * 128, 128), :] for i in range(6)]))

    def merge_right():
        for dx in (1, 2, 3):
            arrive(gr_all.at[aligned(lax.rem(x + dx, 4), 192), :], grr.at[4 + dx])
        tr_h[...], tr_l[...] = split(merged(
            [upper(tr[p]).T for p in range(4)], [gr_all[pl.ds(i * 128, 128), :] for i in range(6)]))

    for o in range(1, 16, 2):
        arrive(yl_slot(o // 4, (o // 2) % 2, 1), ylr.at[o])
    put(ylbuf, yl_out, osem.at[1])
    turn(ylbuf, ylt_h, ylt_l, 16)
    gram(ylt_h, ylt_l, gl)
    gram_left()

    slot = yr_slot(0, 1)
    arrive(slot, yrr.at[1])
    for dy in (1, 3, 2):
        send(slot, slot, yrs.at[3 + dy], yrr.at[((4 - dy) % 4) * 2 + 1], (apos(dy, 0), t))

    across(1)
    in_plane(1)

    for dz in (0, 1):
        for dy in (1, 3, 2):
            arrive(yr_slot(dy, dz), yrr.at[dy * 2 + dz])
    put(yrbuf, yr_out, osem.at[0])
    turn(yrbuf, yrt_h, yrt_l, 8)
    gram(yrt_h, yrt_l, gr)
    send(gr, gr_core, grs.at[0], grr.at[0], (a, vpos(0, 0, 1)))

    gram_right()
    for copy in local_t + [local_u, local_v]:
        copy.wait()
    def right_sums(part):
        begin, width = 2 * STARTS[part], 2 * PARTS[part]
        for o in range(1, 8):
            arrive(vbuf.at[aligned(apos(o // 2, o % 2), 128), pl.ds(begin, width)], vr.at[part, o])
        put(vbuf.at[:, pl.ds(begin, width)], v_out.at[:, pl.ds(begin, width)], osem.at[2 + part])

        def tile(n, carry):
            columns = pl.ds(pl.multiple_of(begin + n * 256, 256), 256)
            high, low = split(vbuf[:, columns])
            spr[columns, :] = three(yrt_h[...], yrt_l[...], high, low).T
            return carry
        lax.fori_loop(0, width // 256, tile, 0)
        half = PARTS[part]
        send(spr.at[pl.ds(pl.multiple_of(begin + (1 - c) * half, 128), half), :],
             core_in.at[pl.ds(STARTS[part], half), :], rs.at[part, 0], rr.at[part, 0], (a, vpos(0, 0, 1)))

    def right_share(part, core, row):
        half = PARTS[part]
        return pl.ds(pl.multiple_of(2 * STARTS[part] + core * half + row * (half // 4), 32), half // 4)

    def left_share(part, row):
        quarter = PARTS[part] // 4
        return pl.ds(pl.multiple_of(STARTS[part] + row * quarter, 32), quarter)

    def inner(part):
        return pl.ds(STARTS[part] // 4, PARTS[part] // 4)

    def right_core(part):
        half = PARTS[part]
        arrive(core_in.at[pl.ds(STARTS[part], half), :], rr.at[part, 0])
        mine = pl.ds(pl.multiple_of(2 * STARTS[part] + c * half, 128), half)
        spr[mine, :] += core_in[pl.ds(STARTS[part], half), :]
        for dx in (1, 3, 2):
            send(spr.at[right_share(part, c, lax.rem(x + dx, 4)), :], x_in.at[(4 - dx) % 4 - 1, inner(part), :],
                 rs.at[part, dx], rr.at[part, (4 - dx) % 4], (a, vpos(dx, 0, 0)))

    def right_pair(part):
        for dx in (1, 2, 3):
            arrive(x_in.at[dx - 1, inner(part), :], rr.at[part, dx])
        at = inner(part)
        shr[at, :] = spr[right_share(part, c, x), :] + x_in[0, at, :] + x_in[1, at, :] + x_in[2, at, :]
        send(shr.at[at, :], zl_in.at[at, :], rs.at[part, 4], rr.at[part, 4], (a, vpos(0, 1, 0)))

    def right_spread(part):
        at = inner(part)
        arrive(zl_in.at[at, :], rr.at[part, 4])
        high, low = split(shr[at, :] + zl_in[at, :])
        place = wr.at[right_share(part, c, x), :]
        place[...] = three(high, low, tr_h[...], tr_l[...], dot_t)
        for dx in (1, 3, 2):
            send(place, place, rs.at[part, 4 + dx], rr.at[part, 4 + (4 - dx) % 4], (a, vpos(dx, 0, 0)))
        send(place, place, rs.at[part, 8], rr.at[part, 8], (a, vpos(0, 0, 1)))

    def right_onward(part):
        for dx in (1, 3, 2):
            got = wr.at[right_share(part, c, lax.rem(x + dx, 4)), :]
            arrive(got, rr.at[part, 4 + dx])
            send(got, got, rs.at[part, 8 + dx], rr.at[part, 8 + dx], (a, vpos(0, 0, 1)))

    def right_done(part):
        for dx in (0, 1, 2, 3):
            arrive(wr.at[right_share(part, 1 - c, lax.rem(x + dx, 4)), :], rr.at[part, 8 + dx])

    def left_sums(part):
        begin, width = STARTS[part], PARTS[part]
        for offset in VERT_OFFSETS:
            arrive(ubuf.at[aligned(vpos(*offset), 128), pl.ds(begin, width)], ur.at[part, flat(offset)])
        put(ubuf.at[:, pl.ds(begin, width)], u_out.at[:, pl.ds(begin, width)], osem.at[4 + part])
        for tile in range(begin, begin + width, 256):
            columns = pl.ds(tile, min(256, begin + width - tile))
            high, low = split(ubuf[:, columns])
            spl[columns, :] = three(ylt_h[...], ylt_l[...], high, low).T
        for dy in (1, 3, 2):
            send(spl.at[left_share(part, lax.rem(y + dy, 4)), :], y_in.at[(4 - dy) % 4 - 1, inner(part), :],
                 ls.at[part, dy], lr.at[part, (4 - dy) % 4], (apos(dy, 0), t))

    def left_pair(part):
        at = inner(part)
        for dy in (1, 2, 3):
            arrive(y_in.at[dy - 1, at, :], lr.at[part, dy])
        shl[at, :] = spl[left_share(part, y), :] + y_in[0, at, :] + y_in[1, at, :] + y_in[2, at, :]
        send(shl.at[at, :], zh_in.at[at, :], ls.at[part, 4], lr.at[part, 4], (apos(0, 1), t))

    def left_spread(part):
        at = inner(part)
        arrive(zh_in.at[at, :], lr.at[part, 4])
        high, low = split(shl[at, :] + zh_in[at, :])
        place = wl.at[left_share(part, y), :]
        place[...] = three(high, low, tl_h[...], tl_l[...], dot_t)
        for dy in (1, 3, 2):
            send(place, place, ls.at[part, 4 + dy], lr.at[part, 4 + (4 - dy) % 4], (apos(dy, 0), t))

    def left_done(part):
        for dy in (1, 2, 3):
            arrive(wl.at[left_share(part, lax.rem(y + dy, 4)), :], lr.at[part, 4 + dy])

    right_sums(0)
    left_sums(0)
    right_core(0)
    gram_pair_right()
    gram_pair_left()
    right_sums(1)
    gram_spread_right()
    gram_spread_left()
    left_sums(1)
    right_core(1)
    merge_right()
    right_pair(0)
    left_pair(0)
    merge_left()
    right_pair(1)
    left_pair(1)
    right_spread(0)
    left_spread(0)
    right_spread(1)
    left_spread(1)
    right_onward(0)
    right_onward(1)
    for part in range(2):
        left_done(part)
        right_done(part)
    put(wr, wr_out, osem.at[6])
    put(wl, wl_out, osem.at[7])
    for copy in sent:
        copy.wait_send()
    for copy in out_copies:
        copy.wait()


def update_kernel(wl, yl, u, yr, v, wr, u_out, v_out, wl_h, wl_l, wr_h, wr_l):
    step = pl.program_id(0)

    @pl.when(step == 0)
    def _():
        wl_h[...], wl_l[...] = split(wl[...])

    @pl.when(step == 4)
    def _():
        wr_h[...], wr_l[...] = split(wr[...])

    @pl.when(step < 4)
    def _():
        high, low = split(yl[...])
        u_out[...] = u[...] - three(high, low, wl_h[...], wl_l[...], dot_t)

    @pl.when(step >= 4)
    def _():
        high, low = split(yr[...])
        v_out[...] = v[...] - three(high, low, wr_h[...], wr_l[...], dot_t)


def shards(u_band, v_band, y_left, t_left, y_right, t_right):
    any_space = pl.BlockSpec(memory_space=pl.ANY)
    shape = jax.ShapeDtypeStruct
    dma = pltpu.SemaphoreType.DMA
    buf = lambda *dims: pltpu.VMEM(dims, f32)
    half = lambda *dims: pltpu.VMEM(dims, bf16)
    u_all, v_all, yl_all, yr_all, w_left, w_right = pl.pallas_call(
        move_kernel,
        out_shape=[
            shape((2048, 512), f32), shape((1024, 1024), f32),
            shape((2048, 512), f32), shape((1024, 512), f32),
            shape((512, 512), f32), shape((1024, 512), f32),
        ],
        in_specs=[any_space] * 6,
        out_specs=[any_space] * 6,
        scratch_shapes=[
            buf(2048, 512), buf(1024, 1024), buf(2048, 512), buf(1024, 512),
            half(512, 2048), half(512, 2048), half(512, 1024), half(512, 1024),
            buf(1024, 512), buf(512, 512), buf(3, 128, 512), buf(128, 512), buf(128, 512), buf(1024, 512),
            buf(512, 512), buf(3, 128, 512), buf(128, 512), buf(128, 512), buf(512, 512),
            buf(768, 128), buf(3, 192, 128), buf(192, 128), buf(192, 128), buf(768, 128),
            buf(768, 128), buf(768, 128), buf(768, 128), buf(3, 192, 128), buf(192, 128), buf(192, 128), buf(768, 128),
            half(512, 512), half(512, 512), half(512, 512), half(512, 512),
            buf(4, 128, 128), buf(4, 128, 128),
            dma((12,)), dma((8,)), dma((16,)), dma((16,)), dma((8,)), dma((8,)),
            dma((len(PARTS), 16)), dma((len(PARTS), 16)), dma((len(PARTS), 8)), dma((len(PARTS), 8)),
            dma((len(PARTS), 12)), dma((len(PARTS), 12)), dma((len(PARTS), 8)), dma((len(PARTS), 8)),
            dma((8,)), dma((8,)), dma((8,)), dma((8,)),
        ],
        compiler_params=pltpu.CompilerParams(
            collective_id=0, has_side_effects=True, vmem_limit_bytes=60 * 2**20,
        ),
        cost_estimate=pl.CostEstimate(flops=2 * 10**10, bytes_accessed=4 * 10**8, transcendentals=0),
    )(y_left, y_right, u_band, v_band, t_left, t_right)

    first = lambda i: (jnp.minimum(i, 3), 0)
    second = lambda i: (jnp.maximum(i - 4, 0), 0)
    whole = lambda i: (0, 0)
    return pl.pallas_call(
        update_kernel,
        grid=(6,),
        out_shape=[shape((2048, 512), f32), shape((1024, 1024), f32)],
        in_specs=[
            pl.BlockSpec((512, 512), whole),
            pl.BlockSpec((512, 512), first), pl.BlockSpec((512, 512), first),
            pl.BlockSpec((512, 512), second), pl.BlockSpec((512, 1024), second),
            pl.BlockSpec((1024, 512), whole),
        ],
        out_specs=[pl.BlockSpec((512, 512), first), pl.BlockSpec((512, 1024), second)],
        scratch_shapes=[half(512, 512), half(512, 512), half(1024, 512), half(1024, 512)],
        compiler_params=pltpu.CompilerParams(vmem_limit_bytes=60 * 2**20),
    )(w_left, yl_all, u_all, yr_all, v_all, w_right)


def solution(mesh):
    return jax.shard_map(
        shards,
        mesh=mesh,
        in_specs=(
            P(("au", "vert"), None),
            P(("vert", "au"), None),
            P(None, ("au", "vert"), None),
            P(),
            P(None, ("vert", "au"), None),
            P(),
        ),
        out_specs=(P("au", "vert"), P("vert", "au")),
        check_vma=False,
    )
```

```python
import functools

import jax
import jax.numpy as jnp
from jax import lax
from jax.experimental import pallas as pl
from jax.experimental.pallas import tpu as pltpu
from jax.sharding import PartitionSpec as P

MESH = pl.DeviceIdType.MESH
f32 = jnp.float32
bf16 = jnp.bfloat16
PARTS = (256, 256)
STARTS = [sum(PARTS[:part]) for part in range(len(PARTS))]
PAIRS = [(0, 1), (0, 2), (0, 3), (1, 2), (1, 3), (2, 3)]
VERT_OFFSETS = [(dx, dz, dc) for dx in (2, 1, 3, 0) for dz in (1, 0) for dc in (0, 1)][:-2] + [(0, 0, 1)]


def split(value):
    high = value.astype(bf16)
    return high, (value - high.astype(f32)).astype(bf16)


def dot(a, b):
    return lax.dot_general(a, b, (((1,), (0,)), ((), ())), preferred_element_type=f32)


def dot_t(a, b):
    return lax.dot_general(a, b, (((1,), (1,)), ((), ())), preferred_element_type=f32)


def three(a_high, a_low, b_high, b_low, product=dot):
    return product(a_high, b_high) + product(a_high, b_low) + product(a_low, b_high)


def exact(a, b):
    return three(*split(a), *split(b))


def aligned(index, size):
    return pl.ds(pl.multiple_of(index * size, size), size)


def flat(offset):
    dx, dz, dc = offset
    return dx * 4 + dz * 2 + dc


def back(offset):
    dx, dz, dc = offset
    return ((4 - dx) % 4, dz, dc)


def merged(*sides):
    rows = [[None] * 4 for _ in sides]
    for p in (3, 2, 1, 0):
        for done, (factors, grams) in zip(rows, sides):
            unit = (lax.broadcasted_iota(jnp.int32, (128, 512), 0) + p * 128
                    == lax.broadcasted_iota(jnp.int32, (128, 512), 1)).astype(f32)
            if p < 3:
                beside = jnp.concatenate([grams[PAIRS.index((p, q))] for q in range(p + 1, 4)], axis=1)
                unit = unit - exact(beside, jnp.concatenate(done[p + 1:], axis=0))
            done[p] = exact(factors[p], unit)
    return [jnp.concatenate(done, axis=0) for done in rows]


def upper(t):
    keep = (lax.broadcasted_iota(jnp.int32, (128, 128), 0)
            <= lax.broadcasted_iota(jnp.int32, (128, 128), 1))
    return jnp.where(keep, t, 0.0)


def move_kernel(
    yl, yr, u, v, tl_in, tr_in,
    u_out, v_out, yl_out, yr_out, wl_out, wr_out,
    ubuf, vbuf, ylbuf, yrbuf, ylt_h, ylt_l, yrt_h, yrt_l,
    spr, core_in, x_in, shr, zl_in, wr,
    spl, y_in, shl, zh_in, wl,
    gl, gl_in, gl_sh, gl_z, gl_all, gr, gr_core, gr_sum, gr_in, gr_sh, gr_z, gr_all,
    tl_h, tl_l, tr_h, tr_l, tl, tr,
    lsem, osem, yls, ylr, yrs, yrr, us, ur, vs, vr,
    rs, rr, ls, lr, gls, glr, grs, grr,
):
    a = lax.axis_index("au")
    t = lax.axis_index("vert")
    y, zh = a // 2, a % 2
    x, zl, c = t // 4, (t // 2) % 2, t % 2

    def vpos(dx, dz, dc):
        return lax.rem(x + dx, 4) * 4 + lax.rem(zl + dz, 2) * 2 + lax.rem(c + dc, 2)

    def apos(dy, dz):
        return lax.rem(y + dy, 4) * 2 + lax.rem(zh + dz, 2)

    sent = []

    def send(src, dst, ssem, rsem, device):
        copy = pltpu.make_async_remote_copy(
            src_ref=src, dst_ref=dst, send_sem=ssem, recv_sem=rsem,
            device_id=device, device_id_type=MESH,
        )
        copy.start()
        sent.append(copy)

    def arrive(dst, sem):
        pltpu.make_async_remote_copy(
            src_ref=dst, dst_ref=dst, send_sem=sem, recv_sem=sem,
            device_id=(a, t), device_id_type=MESH,
        ).wait_recv()

    out_copies = []

    def put(src, dst, sem):
        copy = pltpu.make_async_copy(src, dst, sem)
        copy.start()
        out_copies.append(copy)

    locals_y = []
    for p in range(4):
        locals_y.append(pltpu.make_async_copy(
            yl.at[p], ylbuf.at[aligned(t, 128), pl.ds(p * 128, 128)], lsem.at[p]))
        locals_y.append(pltpu.make_async_copy(
            yr.at[p], yrbuf.at[aligned(a, 128), pl.ds(p * 128, 128)], lsem.at[4 + p]))
    local_u = pltpu.make_async_copy(u.at[:, aligned(t, 512)], ubuf.at[aligned(t, 128), :], lsem.at[8])
    local_v = pltpu.make_async_copy(v.at[:, aligned(a, 1024)], vbuf.at[aligned(a, 128), :], lsem.at[9])
    local_t = [pltpu.make_async_copy(tl_in, tl, lsem.at[10]), pltpu.make_async_copy(tr_in, tr, lsem.at[11])]
    for copy in locals_y + [local_u, local_v] + local_t:
        copy.start()

    barrier = pltpu.get_barrier_semaphore()
    for offset in VERT_OFFSETS:
        pl.semaphore_signal(barrier, inc=1, device_id=(a, vpos(*offset)), device_id_type=MESH)
    for o in range(1, 8):
        pl.semaphore_signal(barrier, inc=1, device_id=(apos(o // 2, o % 2), t), device_id_type=MESH)
    pl.semaphore_wait(barrier, 22)

    for copy in locals_y:
        copy.wait()

    def yl_slot(dx, dz, dc):
        return ylbuf.at[aligned(vpos(dx, dz, dc), 128), :]

    def yr_slot(dy, dz):
        return yrbuf.at[aligned(apos(dy, dz), 128), :]

    def send_v(part, o):
        dy, dz = o // 2, o % 2
        target = apos(dy, dz)
        begin, width = 2 * STARTS[part], 2 * PARTS[part]
        send(v.at[:, pl.ds(pl.multiple_of(target * 1024 + begin, 256), width)],
             vbuf.at[aligned(a, 128), pl.ds(begin, width)],
             vs.at[part, o], vr.at[part, ((4 - dy) % 4) * 2 + dz], (target, t))

    def send_u(part, offset):
        target = vpos(*offset)
        begin, width = STARTS[part], PARTS[part]
        send(u.at[:, pl.ds(pl.multiple_of(target * 512 + begin, 128), width)],
             ubuf.at[aligned(t, 128), pl.ds(begin, width)],
             us.at[part, flat(offset)], ur.at[part, flat(back(offset))], (a, target))

    def in_plane(part):
        for o in (2, 6, 4):
            send_v(part, o)
        for dc in (0, 1):
            for dx in (1, 3, 2):
                send_u(part, (dx, 0, dc))
        send_u(part, (0, 0, 1))

    def across(part):
        for o, dx in ((1, 0), (3, 1), (7, 3), (5, 2)):
            send_v(part, o)
            for dc in (0, 1):
                send_u(part, (dx, 1, dc))

    own = yl_slot(0, 0, 0)
    mine = yr_slot(0, 0)
    send(own, own, yls.at[0], ylr.at[2], (a, vpos(0, 1, 0)))
    send(mine, mine, yrs.at[0], yrr.at[1], (apos(0, 1), t))
    for d in (1, 3, 2):
        send(own, own, yls.at[d], ylr.at[((4 - d) % 4) * 4], (a, vpos(d, 0, 0)))
        send(mine, mine, yrs.at[d], yrr.at[((4 - d) % 4) * 2], (apos(d, 0), t))
    send(own, own, yls.at[7], ylr.at[1], (a, vpos(0, 0, 1)))

    slot = yl_slot(0, 1, 0)
    arrive(slot, ylr.at[2])
    for dx in (1, 3, 2):
        send(slot, slot, yls.at[3 + dx], ylr.at[((4 - dx) % 4) * 4 + 2], (a, vpos(dx, 0, 0)))
    send(slot, slot, yls.at[8], ylr.at[3], (a, vpos(0, 0, 1)))
    across(0)
    in_plane(0)
    for dz in (0, 1):
        for dx in (1, 3, 2):
            slot = yl_slot(dx, dz, 0)
            arrive(slot, ylr.at[dx * 4 + dz * 2])
            send(slot, slot, yls.at[8 + dz * 3 + dx], ylr.at[dx * 4 + dz * 2 + 1], (a, vpos(0, 0, 1)))

    def turn(source, high, low, count):
        def body(j, carry):
            high_part, low_part = split(source[aligned(j, 128), :].T)
            high[:, aligned(j, 128)] = high_part
            low[:, aligned(j, 128)] = low_part
            return carry
        lax.fori_loop(0, count, body, 0)

    def gram(high, low, out):
        def block(p, n, q, m):
            rows, cols = pl.ds(p * 128, n * 128), pl.ds(q * 128, m * 128)
            return three(high[rows, :], low[rows, :], high[cols, :], low[cols, :], dot_t)
        out[0:128, :] = block(0, 1, 1, 1)
        square = block(0, 2, 2, 2)
        out[128:256, :] = square[:128, :128]
        out[256:384, :] = square[:128, 128:]
        out[384:512, :] = square[128:, :128]
        out[512:640, :] = square[128:, 128:]
        out[640:768, :] = block(2, 1, 3, 1)

    def gram_left():
        for dy in (1, 3, 2):
            send(gl.at[aligned(lax.rem(y + dy, 4), 192), :], gl_in.at[(4 - dy) % 4 - 1],
                 gls.at[dy], glr.at[(4 - dy) % 4], (apos(dy, 0), t))

    def gram_right():
        arrive(gr_core, grr.at[0])
        gr_sum[...] = gr[...] + gr_core[...]
        for dx in (1, 3, 2):
            send(gr_sum.at[aligned(lax.rem(x + dx, 4), 192), :], gr_in.at[(4 - dx) % 4 - 1],
                 grs.at[dx], grr.at[(4 - dx) % 4], (a, vpos(dx, 0, 0)))

    def gram_pair_left():
        for dy in (1, 3, 2):
            arrive(gl_in.at[dy - 1], glr.at[dy])
        gl_sh[...] = gl[aligned(y, 192), :] + gl_in[0] + gl_in[1] + gl_in[2]
        send(gl_sh, gl_z, gls.at[4], glr.at[4], (apos(0, 1), t))

    def gram_pair_right():
        for dx in (1, 3, 2):
            arrive(gr_in.at[dx - 1], grr.at[dx])
        gr_sh[...] = gr_sum[aligned(x, 192), :] + gr_in[0] + gr_in[1] + gr_in[2]
        send(gr_sh, gr_z, grs.at[4], grr.at[4], (a, vpos(0, 1, 0)))

    def gram_spread_left():
        arrive(gl_z, glr.at[4])
        spot_l = gl_all.at[aligned(y, 192), :]
        spot_l[...] = gl_sh[...] + gl_z[...]
        for dy in (1, 3, 2):
            send(spot_l, spot_l, gls.at[4 + dy], glr.at[4 + (4 - dy) % 4], (apos(dy, 0), t))

    def gram_spread_right():
        arrive(gr_z, grr.at[4])
        spot_r = gr_all.at[aligned(x, 192), :]
        spot_r[...] = gr_sh[...] + gr_z[...]
        for dx in (1, 3, 2):
            send(spot_r, spot_r, grs.at[4 + dx], grr.at[4 + (4 - dx) % 4], (a, vpos(dx, 0, 0)))

    def merge_both():
        for d in (1, 2, 3):
            arrive(gr_all.at[aligned(lax.rem(x + d, 4), 192), :], grr.at[4 + d])
            arrive(gl_all.at[aligned(lax.rem(y + d, 4), 192), :], glr.at[4 + d])
        right, left = merged(
            ([upper(tr[p]).T for p in range(4)], [gr_all[pl.ds(i * 128, 128), :] for i in range(6)]),
            ([upper(tl[p]) for p in range(4)], [gl_all[pl.ds(i * 128, 128), :] for i in range(6)]),
        )
        tr_h[...], tr_l[...] = split(right)
        tl_h[...], tl_l[...] = split(left)

    for o in range(1, 16, 2):
        arrive(yl_slot(o // 4, (o // 2) % 2, 1), ylr.at[o])
    put(ylbuf, yl_out, osem.at[1])
    turn(ylbuf, ylt_h, ylt_l, 16)
    gram(ylt_h, ylt_l, gl)
    gram_left()

    slot = yr_slot(0, 1)
    arrive(slot, yrr.at[1])
    for dy in (1, 3, 2):
        send(slot, slot, yrs.at[3 + dy], yrr.at[((4 - dy) % 4) * 2 + 1], (apos(dy, 0), t))

    across(1)
    in_plane(1)

    for dz in (0, 1):
        for dy in (1, 3, 2):
            arrive(yr_slot(dy, dz), yrr.at[dy * 2 + dz])
    put(yrbuf, yr_out, osem.at[0])
    turn(yrbuf, yrt_h, yrt_l, 8)
    gram(yrt_h, yrt_l, gr)
    send(gr, gr_core, grs.at[0], grr.at[0], (a, vpos(0, 0, 1)))

    gram_right()
    for copy in local_t + [local_u, local_v]:
        copy.wait()
    def right_sums(part):
        begin, width = 2 * STARTS[part], 2 * PARTS[part]
        for o in range(1, 8):
            arrive(vbuf.at[aligned(apos(o // 2, o % 2), 128), pl.ds(begin, width)], vr.at[part, o])
        put(vbuf.at[:, pl.ds(begin, width)], v_out.at[:, pl.ds(begin, width)], osem.at[2 + part])

        def tile(n, carry):
            columns = pl.ds(pl.multiple_of(begin + n * 256, 256), 256)
            high, low = split(vbuf[:, columns])
            spr[columns, :] = three(yrt_h[...], yrt_l[...], high, low).T
            return carry
        lax.fori_loop(0, width // 256, tile, 0)
        half = PARTS[part]
        send(spr.at[pl.ds(pl.multiple_of(begin + (1 - c) * half, 128), half), :],
             core_in.at[pl.ds(STARTS[part], half), :], rs.at[part, 0], rr.at[part, 0], (a, vpos(0, 0, 1)))

    def right_share(part, core, row):
        half = PARTS[part]
        return pl.ds(pl.multiple_of(2 * STARTS[part] + core * half + row * (half // 4), 32), half // 4)

    def left_share(part, row):
        quarter = PARTS[part] // 4
        return pl.ds(pl.multiple_of(STARTS[part] + row * quarter, 32), quarter)

    def inner(part):
        return pl.ds(STARTS[part] // 4, PARTS[part] // 4)

    def right_core(part):
        half = PARTS[part]
        arrive(core_in.at[pl.ds(STARTS[part], half), :], rr.at[part, 0])
        mine = pl.ds(pl.multiple_of(2 * STARTS[part] + c * half, 128), half)
        spr[mine, :] += core_in[pl.ds(STARTS[part], half), :]
        for dx in (1, 3, 2):
            send(spr.at[right_share(part, c, lax.rem(x + dx, 4)), :], x_in.at[(4 - dx) % 4 - 1, inner(part), :],
                 rs.at[part, dx], rr.at[part, (4 - dx) % 4], (a, vpos(dx, 0, 0)))

    def right_pair(part):
        for dx in (1, 2, 3):
            arrive(x_in.at[dx - 1, inner(part), :], rr.at[part, dx])
        at = inner(part)
        shr[at, :] = spr[right_share(part, c, x), :] + x_in[0, at, :] + x_in[1, at, :] + x_in[2, at, :]
        send(shr.at[at, :], zl_in.at[at, :], rs.at[part, 4], rr.at[part, 4], (a, vpos(0, 1, 0)))

    def right_spread(part):
        at = inner(part)
        arrive(zl_in.at[at, :], rr.at[part, 4])
        high, low = split(shr[at, :] + zl_in[at, :])
        place = wr.at[right_share(part, c, x), :]
        place[...] = three(high, low, tr_h[...], tr_l[...], dot_t)
        for dx in (1, 3, 2):
            send(place, place, rs.at[part, 4 + dx], rr.at[part, 4 + (4 - dx) % 4], (a, vpos(dx, 0, 0)))
        send(place, place, rs.at[part, 8], rr.at[part, 8], (a, vpos(0, 0, 1)))

    def right_onward(part):
        for dx in (1, 3, 2):
            got = wr.at[right_share(part, c, lax.rem(x + dx, 4)), :]
            arrive(got, rr.at[part, 4 + dx])
            send(got, got, rs.at[part, 8 + dx], rr.at[part, 8 + dx], (a, vpos(0, 0, 1)))

    def right_done(part):
        for dx in (0, 1, 2, 3):
            arrive(wr.at[right_share(part, 1 - c, lax.rem(x + dx, 4)), :], rr.at[part, 8 + dx])

    def left_sums(part):
        begin, width = STARTS[part], PARTS[part]
        for offset in VERT_OFFSETS:
            arrive(ubuf.at[aligned(vpos(*offset), 128), pl.ds(begin, width)], ur.at[part, flat(offset)])
        put(ubuf.at[:, pl.ds(begin, width)], u_out.at[:, pl.ds(begin, width)], osem.at[4 + part])
        for tile in range(begin, begin + width, 256):
            columns = pl.ds(tile, min(256, begin + width - tile))
            high, low = split(ubuf[:, columns])
            spl[columns, :] = three(ylt_h[...], ylt_l[...], high, low).T
        for dy in (1, 3, 2):
            send(spl.at[left_share(part, lax.rem(y + dy, 4)), :], y_in.at[(4 - dy) % 4 - 1, inner(part), :],
                 ls.at[part, dy], lr.at[part, (4 - dy) % 4], (apos(dy, 0), t))

    def left_pair(part):
        at = inner(part)
        for dy in (1, 2, 3):
            arrive(y_in.at[dy - 1, at, :], lr.at[part, dy])
        shl[at, :] = spl[left_share(part, y), :] + y_in[0, at, :] + y_in[1, at, :] + y_in[2, at, :]
        send(shl.at[at, :], zh_in.at[at, :], ls.at[part, 4], lr.at[part, 4], (apos(0, 1), t))

    def left_spread(part):
        at = inner(part)
        arrive(zh_in.at[at, :], lr.at[part, 4])
        high, low = split(shl[at, :] + zh_in[at, :])
        place = wl.at[left_share(part, y), :]
        place[...] = three(high, low, tl_h[...], tl_l[...], dot_t)
        for dy in (1, 3, 2):
            send(place, place, ls.at[part, 4 + dy], lr.at[part, 4 + (4 - dy) % 4], (apos(dy, 0), t))

    def left_done(part):
        for dy in (1, 2, 3):
            arrive(wl.at[left_share(part, lax.rem(y + dy, 4)), :], lr.at[part, 4 + dy])

    right_sums(0)
    left_sums(0)
    right_core(0)
    gram_pair_right()
    gram_pair_left()
    right_sums(1)
    gram_spread_right()
    gram_spread_left()
    left_sums(1)
    right_core(1)
    right_pair(0)
    left_pair(0)
    merge_both()
    right_pair(1)
    left_pair(1)
    right_spread(0)
    left_spread(0)
    right_spread(1)
    left_spread(1)
    right_onward(0)
    right_onward(1)
    for part in range(2):
        left_done(part)
        right_done(part)
    put(wr, wr_out, osem.at[6])
    put(wl, wl_out, osem.at[7])
    for copy in sent:
        copy.wait_send()
    for copy in out_copies:
        copy.wait()


def update_kernel(wl, yl, u, yr, v, wr_in, u_out, v_out, wl_h, wl_l, wr_h, wr_l, wr, sem):
    step = pl.program_id(0)
    copy = pltpu.make_async_copy(wr_in, wr, sem)

    @pl.when(step == 0)
    def _():
        copy.start()
        wl_h[...], wl_l[...] = split(wl[...])

    @pl.when(step == 4)
    def _():
        copy.wait()
        wr_h[...], wr_l[...] = split(wr[...])

    @pl.when(step < 4)
    def _():
        high, low = split(yl[...])
        u_out[...] = u[...] - three(high, low, wl_h[...], wl_l[...], dot_t)

    @pl.when(step >= 4)
    def _():
        high, low = split(yr[...])
        v_out[...] = v[...] - three(high, low, wr_h[...], wr_l[...], dot_t)


def shards(u_band, v_band, y_left, t_left, y_right, t_right):
    any_space = pl.BlockSpec(memory_space=pl.ANY)
    shape = jax.ShapeDtypeStruct
    dma = pltpu.SemaphoreType.DMA
    buf = lambda *dims: pltpu.VMEM(dims, f32)
    half = lambda *dims: pltpu.VMEM(dims, bf16)
    u_all, v_all, yl_all, yr_all, w_left, w_right = pl.pallas_call(
        move_kernel,
        out_shape=[
            shape((2048, 512), f32), shape((1024, 1024), f32),
            shape((2048, 512), f32), shape((1024, 512), f32),
            shape((512, 512), f32), shape((1024, 512), f32),
        ],
        in_specs=[any_space] * 6,
        out_specs=[any_space] * 6,
        scratch_shapes=[
            buf(2048, 512), buf(1024, 1024), buf(2048, 512), buf(1024, 512),
            half(512, 2048), half(512, 2048), half(512, 1024), half(512, 1024),
            buf(1024, 512), buf(512, 512), buf(3, 128, 512), buf(128, 512), buf(128, 512), buf(1024, 512),
            buf(512, 512), buf(3, 128, 512), buf(128, 512), buf(128, 512), buf(512, 512),
            buf(768, 128), buf(3, 192, 128), buf(192, 128), buf(192, 128), buf(768, 128),
            buf(768, 128), buf(768, 128), buf(768, 128), buf(3, 192, 128), buf(192, 128), buf(192, 128), buf(768, 128),
            half(512, 512), half(512, 512), half(512, 512), half(512, 512),
            buf(4, 128, 128), buf(4, 128, 128),
            dma((12,)), dma((8,)), dma((16,)), dma((16,)), dma((8,)), dma((8,)),
            dma((len(PARTS), 16)), dma((len(PARTS), 16)), dma((len(PARTS), 8)), dma((len(PARTS), 8)),
            dma((len(PARTS), 12)), dma((len(PARTS), 12)), dma((len(PARTS), 8)), dma((len(PARTS), 8)),
            dma((8,)), dma((8,)), dma((8,)), dma((8,)),
        ],
        compiler_params=pltpu.CompilerParams(
            collective_id=0, has_side_effects=True, vmem_limit_bytes=60 * 2**20,
        ),
        cost_estimate=pl.CostEstimate(flops=2 * 10**10, bytes_accessed=4 * 10**8, transcendentals=0),
    )(y_left, y_right, u_band, v_band, t_left, t_right)

    first = lambda i: (jnp.minimum(i, 3), 0)
    second = lambda i: (jnp.maximum(i - 4, 0), 0)
    whole = lambda i: (0, 0)
    return pl.pallas_call(
        update_kernel,
        grid=(6,),
        out_shape=[shape((2048, 512), f32), shape((1024, 1024), f32)],
        in_specs=[
            pl.BlockSpec((512, 512), whole),
            pl.BlockSpec((512, 512), first), pl.BlockSpec((512, 512), first),
            pl.BlockSpec((512, 512), second), pl.BlockSpec((512, 1024), second),
            any_space,
        ],
        out_specs=[pl.BlockSpec((512, 512), first), pl.BlockSpec((512, 1024), second)],
        scratch_shapes=[half(512, 512), half(512, 512), half(1024, 512), half(1024, 512), buf(1024, 512), dma],
        compiler_params=pltpu.CompilerParams(vmem_limit_bytes=60 * 2**20),
    )(w_left, yl_all, u_all, yr_all, v_all, w_right)


def solution(mesh):
    return jax.shard_map(
        shards,
        mesh=mesh,
        in_specs=(
            P(("au", "vert"), None),
            P(("vert", "au"), None),
            P(None, ("au", "vert"), None),
            P(),
            P(None, ("vert", "au"), None),
            P(),
        ),
        out_specs=(P("au", "vert"), P("vert", "au")),
        check_vma=False,
    )
```

```python
import functools

import jax
import jax.numpy as jnp
from jax import lax
from jax.experimental import pallas as pl
from jax.experimental.pallas import tpu as pltpu
from jax.sharding import PartitionSpec as P

MESH = pl.DeviceIdType.MESH
f32 = jnp.float32
bf16 = jnp.bfloat16
PARTS = (256, 256)
STARTS = [sum(PARTS[:part]) for part in range(len(PARTS))]
PAIRS = [(0, 1), (0, 2), (0, 3), (1, 2), (1, 3), (2, 3)]
VERT_OFFSETS = [(dx, dz, dc) for dx in (2, 1, 3, 0) for dz in (1, 0) for dc in (0, 1)][:-2] + [(0, 0, 1)]


def split(value):
    high = value.astype(bf16)
    return high, (value - high.astype(f32)).astype(bf16)


def dot(a, b):
    return lax.dot_general(a, b, (((1,), (0,)), ((), ())), preferred_element_type=f32)


def dot_t(a, b):
    return lax.dot_general(a, b, (((1,), (1,)), ((), ())), preferred_element_type=f32)


def three(a_high, a_low, b_high, b_low, product=dot):
    return product(a_high, b_high) + product(a_high, b_low) + product(a_low, b_high)


def exact(a, b):
    return three(*split(a), *split(b))


def aligned(index, size):
    return pl.ds(pl.multiple_of(index * size, size), size)


def flat(offset):
    dx, dz, dc = offset
    return dx * 4 + dz * 2 + dc


def back(offset):
    dx, dz, dc = offset
    return ((4 - dx) % 4, dz, dc)


def merged(*sides):
    rows = [[None] * 4 for _ in sides]
    for p in (3, 2, 1, 0):
        for done, (factors, grams) in zip(rows, sides):
            unit = (lax.broadcasted_iota(jnp.int32, (128, 512), 0) + p * 128
                    == lax.broadcasted_iota(jnp.int32, (128, 512), 1)).astype(f32)
            if p < 3:
                beside = jnp.concatenate([grams[PAIRS.index((p, q))] for q in range(p + 1, 4)], axis=1)
                unit = unit - exact(beside, jnp.concatenate(done[p + 1:], axis=0))
            done[p] = exact(factors[p], unit)
    return [jnp.concatenate(done, axis=0) for done in rows]


def upper(t):
    keep = (lax.broadcasted_iota(jnp.int32, (128, 128), 0)
            <= lax.broadcasted_iota(jnp.int32, (128, 128), 1))
    return jnp.where(keep, t, 0.0)


def move_kernel(
    yl, yr, u, v, tl_in, tr_in,
    u_out, v_out, yl_out, yr_out, wl_out, wr_out,
    ubuf, vbuf, ylbuf, yrbuf, ylt_h, ylt_l, yrt_h, yrt_l,
    spr, core_in, x_in, shr, zl_in, wr,
    spl, y_in, shl, zh_in, wl,
    gl, gl_in, gl_sh, gl_z, gl_all, gr, gr_core, gr_sum, gr_in, gr_sh, gr_z, gr_all,
    tl_h, tl_l, tr_h, tr_l, tl, tr,
    lsem, osem, yls, ylr, yrs, yrr, us, ur, vs, vr,
    rs, rr, ls, lr, gls, glr, grs, grr,
):
    a = lax.axis_index("au")
    t = lax.axis_index("vert")
    y, zh = a // 2, a % 2
    x, zl, c = t // 4, (t // 2) % 2, t % 2

    def vpos(dx, dz, dc):
        return lax.rem(x + dx, 4) * 4 + lax.rem(zl + dz, 2) * 2 + lax.rem(c + dc, 2)

    def apos(dy, dz):
        return lax.rem(y + dy, 4) * 2 + lax.rem(zh + dz, 2)

    sent = []

    def send(src, dst, ssem, rsem, device):
        copy = pltpu.make_async_remote_copy(
            src_ref=src, dst_ref=dst, send_sem=ssem, recv_sem=rsem,
            device_id=device, device_id_type=MESH,
        )
        copy.start()
        sent.append(copy)

    def arrive(dst, sem):
        pltpu.make_async_remote_copy(
            src_ref=dst, dst_ref=dst, send_sem=sem, recv_sem=sem,
            device_id=(a, t), device_id_type=MESH,
        ).wait_recv()

    out_copies = []

    def put(src, dst, sem):
        copy = pltpu.make_async_copy(src, dst, sem)
        copy.start()
        out_copies.append(copy)

    locals_y = []
    for p in range(4):
        locals_y.append(pltpu.make_async_copy(
            yl.at[p], ylbuf.at[aligned(t, 128), pl.ds(p * 128, 128)], lsem.at[p]))
        locals_y.append(pltpu.make_async_copy(
            yr.at[p], yrbuf.at[aligned(a, 128), pl.ds(p * 128, 128)], lsem.at[4 + p]))
    local_u = pltpu.make_async_copy(u.at[:, aligned(t, 512)], ubuf.at[aligned(t, 128), :], lsem.at[8])
    local_v = pltpu.make_async_copy(v.at[:, aligned(a, 1024)], vbuf.at[aligned(a, 128), :], lsem.at[9])
    local_t = [pltpu.make_async_copy(tl_in, tl, lsem.at[10]), pltpu.make_async_copy(tr_in, tr, lsem.at[11])]
    for copy in locals_y + [local_u, local_v] + local_t:
        copy.start()

    barrier = pltpu.get_barrier_semaphore()
    for offset in VERT_OFFSETS:
        pl.semaphore_signal(barrier, inc=1, device_id=(a, vpos(*offset)), device_id_type=MESH)
    for o in range(1, 8):
        pl.semaphore_signal(barrier, inc=1, device_id=(apos(o // 2, o % 2), t), device_id_type=MESH)
    pl.semaphore_wait(barrier, 22)

    for copy in locals_y:
        copy.wait()

    def yl_slot(dx, dz, dc):
        return ylbuf.at[aligned(vpos(dx, dz, dc), 128), :]

    def yr_slot(dy, dz):
        return yrbuf.at[aligned(apos(dy, dz), 128), :]

    def send_v(part, o):
        dy, dz = o // 2, o % 2
        target = apos(dy, dz)
        begin, width = 2 * STARTS[part], 2 * PARTS[part]
        send(v.at[:, pl.ds(pl.multiple_of(target * 1024 + begin, 256), width)],
             vbuf.at[aligned(a, 128), pl.ds(begin, width)],
             vs.at[part, o], vr.at[part, ((4 - dy) % 4) * 2 + dz], (target, t))

    def send_u(part, offset):
        target = vpos(*offset)
        begin, width = STARTS[part], PARTS[part]
        send(u.at[:, pl.ds(pl.multiple_of(target * 512 + begin, 128), width)],
             ubuf.at[aligned(t, 128), pl.ds(begin, width)],
             us.at[part, flat(offset)], ur.at[part, flat(back(offset))], (a, target))

    def in_plane(part):
        for o in (2, 6, 4):
            send_v(part, o)
        for dc in (0, 1):
            for dx in (1, 3, 2):
                send_u(part, (dx, 0, dc))
        send_u(part, (0, 0, 1))

    def across(part):
        for o, dx in ((1, 0), (3, 1), (7, 3), (5, 2)):
            send_v(part, o)
            for dc in (0, 1):
                send_u(part, (dx, 1, dc))

    own = yl_slot(0, 0, 0)
    mine = yr_slot(0, 0)
    send(own, own, yls.at[0], ylr.at[2], (a, vpos(0, 1, 0)))
    send(mine, mine, yrs.at[0], yrr.at[1], (apos(0, 1), t))
    for d in (1, 3, 2):
        send(own, own, yls.at[d], ylr.at[((4 - d) % 4) * 4], (a, vpos(d, 0, 0)))
        send(mine, mine, yrs.at[d], yrr.at[((4 - d) % 4) * 2], (apos(d, 0), t))
    send(own, own, yls.at[7], ylr.at[1], (a, vpos(0, 0, 1)))

    slot = yl_slot(0, 1, 0)
    arrive(slot, ylr.at[2])
    for dx in (1, 3, 2):
        send(slot, slot, yls.at[3 + dx], ylr.at[((4 - dx) % 4) * 4 + 2], (a, vpos(dx, 0, 0)))
    send(slot, slot, yls.at[8], ylr.at[3], (a, vpos(0, 0, 1)))
    across(0)
    in_plane(0)
    for dz in (0, 1):
        for dx in (1, 3, 2):
            slot = yl_slot(dx, dz, 0)
            arrive(slot, ylr.at[dx * 4 + dz * 2])
            send(slot, slot, yls.at[8 + dz * 3 + dx], ylr.at[dx * 4 + dz * 2 + 1], (a, vpos(0, 0, 1)))

    def turn(source, high, low, count):
        def body(j, carry):
            high_part, low_part = split(source[aligned(j, 128), :].T)
            high[:, aligned(j, 128)] = high_part
            low[:, aligned(j, 128)] = low_part
            return carry
        lax.fori_loop(0, count, body, 0)

    def gram(high, low, out):
        def block(p, n, q, m):
            rows, cols = pl.ds(p * 128, n * 128), pl.ds(q * 128, m * 128)
            return three(high[rows, :], low[rows, :], high[cols, :], low[cols, :], dot_t)
        out[0:128, :] = block(0, 1, 1, 1)
        square = block(0, 2, 2, 2)
        out[128:256, :] = square[:128, :128]
        out[256:384, :] = square[:128, 128:]
        out[384:512, :] = square[128:, :128]
        out[512:640, :] = square[128:, 128:]
        out[640:768, :] = block(2, 1, 3, 1)

    def gram_left():
        for dy in (1, 3, 2):
            send(gl.at[aligned(lax.rem(y + dy, 4), 192), :], gl_in.at[(4 - dy) % 4 - 1],
                 gls.at[dy], glr.at[(4 - dy) % 4], (apos(dy, 0), t))

    def gram_right():
        arrive(gr_core, grr.at[0])
        gr_sum[...] = gr[...] + gr_core[...]
        for dx in (1, 3, 2):
            send(gr_sum.at[aligned(lax.rem(x + dx, 4), 192), :], gr_in.at[(4 - dx) % 4 - 1],
                 grs.at[dx], grr.at[(4 - dx) % 4], (a, vpos(dx, 0, 0)))

    def gram_pair_left():
        for dy in (1, 3, 2):
            arrive(gl_in.at[dy - 1], glr.at[dy])
        gl_sh[...] = gl[aligned(y, 192), :] + gl_in[0] + gl_in[1] + gl_in[2]
        send(gl_sh, gl_z, gls.at[4], glr.at[4], (apos(0, 1), t))

    def gram_pair_right():
        for dx in (1, 3, 2):
            arrive(gr_in.at[dx - 1], grr.at[dx])
        gr_sh[...] = gr_sum[aligned(x, 192), :] + gr_in[0] + gr_in[1] + gr_in[2]
        send(gr_sh, gr_z, grs.at[4], grr.at[4], (a, vpos(0, 1, 0)))

    def gram_spread_left():
        arrive(gl_z, glr.at[4])
        spot_l = gl_all.at[aligned(y, 192), :]
        spot_l[...] = gl_sh[...] + gl_z[...]
        for dy in (1, 3, 2):
            send(spot_l, spot_l, gls.at[4 + dy], glr.at[4 + (4 - dy) % 4], (apos(dy, 0), t))

    def gram_spread_right():
        arrive(gr_z, grr.at[4])
        spot_r = gr_all.at[aligned(x, 192), :]
        spot_r[...] = gr_sh[...] + gr_z[...]
        for dx in (1, 3, 2):
            send(spot_r, spot_r, grs.at[4 + dx], grr.at[4 + (4 - dx) % 4], (a, vpos(dx, 0, 0)))

    def merge_both():
        for d in (1, 2, 3):
            arrive(gr_all.at[aligned(lax.rem(x + d, 4), 192), :], grr.at[4 + d])
            arrive(gl_all.at[aligned(lax.rem(y + d, 4), 192), :], glr.at[4 + d])
        right, left = merged(
            ([upper(tr[p]).T for p in range(4)], [gr_all[pl.ds(i * 128, 128), :] for i in range(6)]),
            ([upper(tl[p]) for p in range(4)], [gl_all[pl.ds(i * 128, 128), :] for i in range(6)]),
        )
        tr_h[...], tr_l[...] = split(right)
        tl_h[...], tl_l[...] = split(left)

    for o in range(1, 16, 2):
        arrive(yl_slot(o // 4, (o // 2) % 2, 1), ylr.at[o])
    put(ylbuf, yl_out, osem.at[1])
    turn(ylbuf, ylt_h, ylt_l, 16)
    gram(ylt_h, ylt_l, gl)
    gram_left()

    slot = yr_slot(0, 1)
    arrive(slot, yrr.at[1])
    for dy in (1, 3, 2):
        send(slot, slot, yrs.at[3 + dy], yrr.at[((4 - dy) % 4) * 2 + 1], (apos(dy, 0), t))

    across(1)
    in_plane(1)

    for dz in (0, 1):
        for dy in (1, 3, 2):
            arrive(yr_slot(dy, dz), yrr.at[dy * 2 + dz])
    put(yrbuf, yr_out, osem.at[0])
    turn(yrbuf, yrt_h, yrt_l, 8)
    gram(yrt_h, yrt_l, gr)
    send(gr, gr_core, grs.at[0], grr.at[0], (a, vpos(0, 0, 1)))

    gram_right()
    for copy in local_t + [local_u, local_v]:
        copy.wait()
    def right_sums(part):
        begin, width = 2 * STARTS[part], 2 * PARTS[part]
        for o in range(1, 8):
            arrive(vbuf.at[aligned(apos(o // 2, o % 2), 128), pl.ds(begin, width)], vr.at[part, o])
        put(vbuf.at[:, pl.ds(begin, width)], v_out.at[:, pl.ds(begin, width)], osem.at[2 + part])

        def tile(n, carry):
            columns = pl.ds(pl.multiple_of(begin + n * 256, 256), 256)
            high, low = split(vbuf[:, columns])
            spr[columns, :] = three(yrt_h[...], yrt_l[...], high, low).T
            return carry
        lax.fori_loop(0, width // 256, tile, 0)
        half = PARTS[part]
        send(spr.at[pl.ds(pl.multiple_of(begin + (1 - c) * half, 128), half), :],
             core_in.at[pl.ds(STARTS[part], half), :], rs.at[part, 0], rr.at[part, 0], (a, vpos(0, 0, 1)))

    def right_share(part, core, row):
        half = PARTS[part]
        return pl.ds(pl.multiple_of(2 * STARTS[part] + core * half + row * (half // 4), 32), half // 4)

    def left_share(part, row):
        quarter = PARTS[part] // 4
        return pl.ds(pl.multiple_of(STARTS[part] + row * quarter, 32), quarter)

    def inner(part):
        return pl.ds(STARTS[part] // 4, PARTS[part] // 4)

    def right_core(part):
        half = PARTS[part]
        arrive(core_in.at[pl.ds(STARTS[part], half), :], rr.at[part, 0])
        mine = pl.ds(pl.multiple_of(2 * STARTS[part] + c * half, 128), half)
        spr[mine, :] += core_in[pl.ds(STARTS[part], half), :]
        for dx in (1, 3, 2):
            send(spr.at[right_share(part, c, lax.rem(x + dx, 4)), :], x_in.at[(4 - dx) % 4 - 1, inner(part), :],
                 rs.at[part, dx], rr.at[part, (4 - dx) % 4], (a, vpos(dx, 0, 0)))

    def right_pair(part):
        for dx in (1, 2, 3):
            arrive(x_in.at[dx - 1, inner(part), :], rr.at[part, dx])
        at = inner(part)
        shr[at, :] = spr[right_share(part, c, x), :] + x_in[0, at, :] + x_in[1, at, :] + x_in[2, at, :]
        send(shr.at[at, :], zl_in.at[at, :], rs.at[part, 4], rr.at[part, 4], (a, vpos(0, 1, 0)))

    def right_spread(part):
        at = inner(part)
        arrive(zl_in.at[at, :], rr.at[part, 4])
        high, low = split(shr[at, :] + zl_in[at, :])
        place = wr.at[right_share(part, c, x), :]
        place[...] = three(high, low, tr_h[...], tr_l[...], dot_t)
        for dx in (1, 3, 2):
            send(place, place, rs.at[part, 4 + dx], rr.at[part, 4 + (4 - dx) % 4], (a, vpos(dx, 0, 0)))
        send(place, place, rs.at[part, 8], rr.at[part, 8], (a, vpos(0, 0, 1)))

    def right_onward(part):
        for dx in (1, 3, 2):
            got = wr.at[right_share(part, c, lax.rem(x + dx, 4)), :]
            arrive(got, rr.at[part, 4 + dx])
            send(got, got, rs.at[part, 8 + dx], rr.at[part, 8 + dx], (a, vpos(0, 0, 1)))

    def right_done(part):
        for dx in (0, 1, 2, 3):
            arrive(wr.at[right_share(part, 1 - c, lax.rem(x + dx, 4)), :], rr.at[part, 8 + dx])

    def left_sums(part):
        begin, width = STARTS[part], PARTS[part]
        for offset in VERT_OFFSETS:
            arrive(ubuf.at[aligned(vpos(*offset), 128), pl.ds(begin, width)], ur.at[part, flat(offset)])
        put(ubuf.at[:, pl.ds(begin, width)], u_out.at[:, pl.ds(begin, width)], osem.at[4 + part])
        for tile in range(begin, begin + width, 256):
            columns = pl.ds(tile, min(256, begin + width - tile))
            high, low = split(ubuf[:, columns])
            spl[columns, :] = three(ylt_h[...], ylt_l[...], high, low).T
        for dy in (1, 3, 2):
            send(spl.at[left_share(part, lax.rem(y + dy, 4)), :], y_in.at[(4 - dy) % 4 - 1, inner(part), :],
                 ls.at[part, dy], lr.at[part, (4 - dy) % 4], (apos(dy, 0), t))

    def left_pair(part):
        at = inner(part)
        for dy in (1, 2, 3):
            arrive(y_in.at[dy - 1, at, :], lr.at[part, dy])
        shl[at, :] = spl[left_share(part, y), :] + y_in[0, at, :] + y_in[1, at, :] + y_in[2, at, :]
        send(shl.at[at, :], zh_in.at[at, :], ls.at[part, 4], lr.at[part, 4], (apos(0, 1), t))

    def left_spread(part):
        at = inner(part)
        arrive(zh_in.at[at, :], lr.at[part, 4])
        high, low = split(shl[at, :] + zh_in[at, :])
        place = wl.at[left_share(part, y), :]
        place[...] = three(high, low, tl_h[...], tl_l[...], dot_t)
        for dy in (1, 3, 2):
            send(place, place, ls.at[part, 4 + dy], lr.at[part, 4 + (4 - dy) % 4], (apos(dy, 0), t))

    def left_done(part):
        for dy in (1, 2, 3):
            arrive(wl.at[left_share(part, lax.rem(y + dy, 4)), :], lr.at[part, 4 + dy])

    right_sums(0)
    left_sums(0)
    right_core(0)
    gram_pair_right()
    gram_pair_left()
    right_sums(1)
    gram_spread_right()
    left_sums(1)
    gram_spread_left()
    right_core(1)
    right_pair(0)
    left_pair(0)
    merge_both()
    right_pair(1)
    left_pair(1)
    right_spread(0)
    left_spread(0)
    right_spread(1)
    left_spread(1)
    right_onward(0)
    right_onward(1)
    for part in range(2):
        left_done(part)
        right_done(part)
    put(wr, wr_out, osem.at[6])
    put(wl, wl_out, osem.at[7])
    for copy in sent:
        copy.wait_send()
    for copy in out_copies:
        copy.wait()


def update_kernel(wl, yl, u, yr, v, wr_in, u_out, v_out, wl_h, wl_l, wr_h, wr_l, wr, sem):
    step = pl.program_id(0)
    copy = pltpu.make_async_copy(wr_in, wr, sem)

    @pl.when(step == 0)
    def _():
        copy.start()
        wl_h[...], wl_l[...] = split(wl[...])

    @pl.when(step == 4)
    def _():
        copy.wait()
        wr_h[...], wr_l[...] = split(wr[...])

    @pl.when(step < 4)
    def _():
        high, low = split(yl[...])
        u_out[...] = u[...] - three(high, low, wl_h[...], wl_l[...], dot_t)

    @pl.when(step >= 4)
    def _():
        high, low = split(yr[...])
        v_out[...] = v[...] - three(high, low, wr_h[...], wr_l[...], dot_t)


def shards(u_band, v_band, y_left, t_left, y_right, t_right):
    any_space = pl.BlockSpec(memory_space=pl.ANY)
    shape = jax.ShapeDtypeStruct
    dma = pltpu.SemaphoreType.DMA
    buf = lambda *dims: pltpu.VMEM(dims, f32)
    half = lambda *dims: pltpu.VMEM(dims, bf16)
    u_all, v_all, yl_all, yr_all, w_left, w_right = pl.pallas_call(
        move_kernel,
        out_shape=[
            shape((2048, 512), f32), shape((1024, 1024), f32),
            shape((2048, 512), f32), shape((1024, 512), f32),
            shape((512, 512), f32), shape((1024, 512), f32),
        ],
        in_specs=[any_space] * 6,
        out_specs=[any_space] * 6,
        scratch_shapes=[
            buf(2048, 512), buf(1024, 1024), buf(2048, 512), buf(1024, 512),
            half(512, 2048), half(512, 2048), half(512, 1024), half(512, 1024),
            buf(1024, 512), buf(512, 512), buf(3, 128, 512), buf(128, 512), buf(128, 512), buf(1024, 512),
            buf(512, 512), buf(3, 128, 512), buf(128, 512), buf(128, 512), buf(512, 512),
            buf(768, 128), buf(3, 192, 128), buf(192, 128), buf(192, 128), buf(768, 128),
            buf(768, 128), buf(768, 128), buf(768, 128), buf(3, 192, 128), buf(192, 128), buf(192, 128), buf(768, 128),
            half(512, 512), half(512, 512), half(512, 512), half(512, 512),
            buf(4, 128, 128), buf(4, 128, 128),
            dma((12,)), dma((8,)), dma((16,)), dma((16,)), dma((8,)), dma((8,)),
            dma((len(PARTS), 16)), dma((len(PARTS), 16)), dma((len(PARTS), 8)), dma((len(PARTS), 8)),
            dma((len(PARTS), 12)), dma((len(PARTS), 12)), dma((len(PARTS), 8)), dma((len(PARTS), 8)),
            dma((8,)), dma((8,)), dma((8,)), dma((8,)),
        ],
        compiler_params=pltpu.CompilerParams(
            collective_id=0, has_side_effects=True, vmem_limit_bytes=60 * 2**20,
        ),
        cost_estimate=pl.CostEstimate(flops=2 * 10**10, bytes_accessed=4 * 10**8, transcendentals=0),
    )(y_left, y_right, u_band, v_band, t_left, t_right)

    first = lambda i: (jnp.minimum(i, 3), 0)
    second = lambda i: (jnp.maximum(i - 4, 0), 0)
    whole = lambda i: (0, 0)
    return pl.pallas_call(
        update_kernel,
        grid=(6,),
        out_shape=[shape((2048, 512), f32), shape((1024, 1024), f32)],
        in_specs=[
            pl.BlockSpec((512, 512), whole),
            pl.BlockSpec((512, 512), first), pl.BlockSpec((512, 512), first),
            pl.BlockSpec((512, 512), second), pl.BlockSpec((512, 1024), second),
            any_space,
        ],
        out_specs=[pl.BlockSpec((512, 512), first), pl.BlockSpec((512, 1024), second)],
        scratch_shapes=[half(512, 512), half(512, 512), half(1024, 512), half(1024, 512), buf(1024, 512), dma],
        compiler_params=pltpu.CompilerParams(vmem_limit_bytes=60 * 2**20),
    )(w_left, yl_all, u_all, yr_all, v_all, w_right)


def solution(mesh):
    return jax.shard_map(
        shards,
        mesh=mesh,
        in_specs=(
            P(("au", "vert"), None),
            P(("vert", "au"), None),
            P(None, ("au", "vert"), None),
            P(),
            P(None, ("vert", "au"), None),
            P(),
        ),
        out_specs=(P("au", "vert"), P("vert", "au")),
        check_vma=False,
    )
```
